512 devices in a mesh: inner: 32 (over x, y), outer: 16 (over z, core).
Axes of the slice: x: 4, y: 8, z: 8, core: 2. Of those that a mesh axis runs over, the one named last changes fastest.
Arguments:
- grad_first: bfloat16 [16, 32, 32, 16, 6, 128], P('outer', 'inner'), may hold values from -1 to 1
- grad_second: bfloat16 [16, 32, 32, 16, 6, 128], P('outer', 'inner'), may hold values from -1 to 1
- master: float32 [2, 32, 16, 6, 128], P(None, 'inner', 'outer'), may hold values from -0.12 to 0.12
- first_moment: float32 [2, 32, 16, 6, 128], P(None, 'inner', 'outer'), may hold values from -1.2 to 1.2
- second_moment: float32 [2, 32, 16, 6, 128], P(None, 'inner', 'outer'), may hold values from 0.01 to 1
Outputs:
- new_master: float32 [2, 32, 16, 6, 128], P(None, 'inner', 'outer')
- new_first: float32 [2, 32, 16, 6, 128], P(None, 'inner', 'outer')
- new_second: float32 [2, 32, 16, 6, 128], P(None, 'inner', 'outer')
- weight_codes: bfloat16 [2, 32, 16, 6, 128], P(None, None, 'outer')
- weight_scales: bfloat16 [2, 32, 16, 6], P(None, None, 'outer')
The draws below stay inside these ranges and needn't reach their ends.
All inputs are finite; a program needn't handle non-finite values.
Results may differ from the reference program's by a relative error of at most 0.012.
Values may be sent and summed in bfloat16 or wider, within the bound.
No kernel may reach another device: no remote copies, remote signals or barrier semaphores. Data moves between devices by JAX's collectives and lax.ppermute only.
A program may use at most 64 MiB of HBM per device.

```python
import math
import jax
import jax.numpy as jnp
from jax import lax

QB = 128
ROWS_DEV = 6
N_INNER = 32
N_OUTER = 16


def spread_blocks(key, spike):
    shape = (N_OUTER, N_INNER, N_INNER, N_OUTER, ROWS_DEV, QB)
    base = jax.random.normal(jax.random.fold_in(key, 11), shape, jnp.float32)
    order = jax.random.permutation(jax.random.fold_in(key, 12), N_INNER)
    paired = (order[:, None] == jnp.arange(N_INNER)[None, :]).astype(jnp.float32)
    factor = 1.0 + (spike - 1.0) * paired
    values = base * factor[None, :, :, None, None, None] * (N_INNER * N_OUTER) ** (-0.5)
    return jnp.clip(values, -1.0, 1.0)


def draw_grad_first(key, part):
    key = jax.random.fold_in(key, 1)
    return spread_blocks(key, 4.0).astype(jnp.bfloat16)


def draw_grad_second(key, part):
    key = jax.random.fold_in(key, 2)
    return spread_blocks(key, 4.0).astype(jnp.bfloat16)


def level_of(key, extent, split, least, high):
    level = 1.0
    for position, blocks in split:
        draws = jax.random.uniform(jax.random.fold_in(jax.random.fold_in(key, 6), position), (blocks,), jnp.float32, least / len(split), high / len(split))
        level = level * jnp.repeat(jnp.exp(draws), extent[position] // blocks).reshape((-1,) + (1,) * (len(extent) - 1 - position))
    return level


def normal_values(rng, dims, deviation, most, split=(), kind=jnp.bfloat16):
    entries = jax.random.normal(rng, dims, jnp.float32) * deviation
    if len(split) > 0:
        entries = level_of(rng, dims, split, -0.22, 0.18) * entries
    return jnp.clip(entries, min=-most, max=most).astype(kind)


def setup_inputs(seed: int = 0) -> dict:
    keys = jax.random.split(jax.random.key(seed), 6)
    return {
        "grad_first": draw_grad_first(jax.random.fold_in(keys[5], 71), 0),
        "grad_second": draw_grad_second(jax.random.fold_in(keys[5], 71), 0),
        "master": normal_values(keys[2], (2, N_INNER, N_OUTER, ROWS_DEV, QB), 0.02, 0.12, ((1, 32), (2, 16)), jnp.float32),
        "first_moment": normal_values(keys[3], (2, N_INNER, N_OUTER, ROWS_DEV, QB), 0.2, 1.2, ((1, 32), (2, 16)), jnp.float32),
        "second_moment": jnp.clip(jnp.exp(math.log(1.0) - 4.6051702 * jax.random.uniform(keys[4], (2, N_INNER, N_OUTER, ROWS_DEV, QB), jnp.float32) ** level_of(keys[4], (2, N_INNER, N_OUTER, ROWS_DEV, QB), ((1, 32), (2, 16)), -0.2, 0.2)), 0.01, 1.0),
    }


EPSILON = 1e-06
CODE_RANGE = 448.0
BETA_ONE = 0.9
BETA_TWO = 0.95
LEARN_RATE = 0.01
WEIGHT_DECAY = 0.1
ADAM_EPSILON = 1e-08
steps_done = 10.0

def quantize(values):
    widened = values.astype(jnp.float32)
    block_scale = ((lax.optimization_barrier(jnp.max(jnp.abs(widened), axis=-1)) + EPSILON) / CODE_RANGE).astype(jnp.bfloat16)
    quant_codes = (widened / block_scale.astype(jnp.float32)[..., None]).astype(jnp.bfloat16)
    return (quant_codes, block_scale)

def restore(quant_codes, block_scale):
    return quant_codes.astype(jnp.float32) * block_scale.astype(jnp.float32)[..., None]

def adamw(reduced, params, first, second):
    first_next = BETA_ONE * first + (1.0 - BETA_ONE) * reduced
    second_next = BETA_TWO * second + (1.0 - BETA_TWO) * reduced * reduced
    first_hat = first_next / (1.0 - BETA_ONE ** steps_done)
    second_hat = second_next / (1.0 - BETA_TWO ** steps_done)
    params_next = params - LEARN_RATE * (first_hat / (jnp.sqrt(second_hat) + ADAM_EPSILON) + WEIGHT_DECAY * params)
    return (params_next, first_next, second_next)

def group_partial(group_grads):
    quant_codes, block_scale = quantize(group_grads)
    return lax.optimization_barrier(jnp.sum(restore(quant_codes, block_scale), axis=0))

def reference(grad_first, grad_second, master, first_moment, second_moment):
    masters, firsts, seconds, all_codes, all_scales = ([], [], [], [], [])
    for bucket, gradient in enumerate((grad_first, grad_second)):
        partials = lax.map(group_partial, gradient)
        codes_two, scale_two = quantize(partials)
        reduced = lax.optimization_barrier(jnp.sum(restore(codes_two, scale_two), axis=0))
        params_next, first_next, second_next = adamw(reduced, master[bucket], first_moment[bucket], second_moment[bucket])
        weight_code, weight_scale = quantize(params_next)
        masters.append(params_next)
        firsts.append(first_next)
        seconds.append(second_next)
        all_codes.append(weight_code)
        all_scales.append(weight_scale)
    return (jnp.stack(masters), jnp.stack(firsts), jnp.stack(seconds), jnp.stack(all_codes), jnp.stack(all_scales))
```

```python
import jax
import jax.numpy as jnp
from jax import lax
from jax.sharding import PartitionSpec as P

EPSILON = 1e-06
CODE_RANGE = 448.0
BETA_ONE = 0.9
BETA_TWO = 0.95
LEARN_RATE = 0.01
WEIGHT_DECAY = 0.1
ADAM_EPSILON = 1e-08
steps_done = 10.0


def quantize(values):
    block_scale = ((jnp.max(jnp.abs(values), axis=-1) + EPSILON) / CODE_RANGE).astype(jnp.bfloat16)
    quant_codes = (values / block_scale.astype(jnp.float32)[..., None]).astype(jnp.bfloat16)
    return (quant_codes, block_scale)


def adamw(reduced, params, first, second):
    first_next = BETA_ONE * first + (1.0 - BETA_ONE) * reduced
    second_next = BETA_TWO * second + (1.0 - BETA_TWO) * reduced * reduced
    first_hat = first_next / (1.0 - BETA_ONE**steps_done)
    second_hat = second_next / (1.0 - BETA_TWO**steps_done)
    params_next = params - LEARN_RATE * (
        first_hat / (jnp.sqrt(second_hat) + ADAM_EPSILON) + WEIGHT_DECAY * params
    )
    return (params_next, first_next, second_next)


def local(grad_first, grad_second, master, first_moment, second_moment):
    _, _, inner, outer, rows, width = grad_first.shape
    every = inner * outer
    sent = jnp.concatenate(
        [g.reshape(every, rows, width) for g in (grad_first, grad_second)], axis=1
    )
    held = lax.all_to_all(sent, ("inner", "outer"), 0, 0, tiled=True)
    reduced = jnp.sum(held.astype(jnp.float32), axis=0).reshape(2, rows, width)
    params_next, first_next, second_next = adamw(
        reduced, master[:, 0, 0], first_moment[:, 0, 0], second_moment[:, 0, 0]
    )
    weight_code, weight_scale = quantize(params_next)
    scale_row = jnp.pad(weight_scale.reshape(1, 2 * rows), ((0, 0), (0, width - 2 * rows)))
    packed = jnp.concatenate([weight_code.reshape(2 * rows, width), scale_row], axis=0)
    spread = jnp.broadcast_to(packed[None], (inner,) + packed.shape)
    group = lax.all_to_all(spread, "inner", 0, 0, tiled=True)
    group_codes = group[:, : 2 * rows].reshape(inner, 2, rows, width).transpose(1, 0, 2, 3)
    group_scales = group[:, 2 * rows, : 2 * rows].reshape(inner, 2, rows).transpose(1, 0, 2)
    return (
        params_next[:, None, None],
        first_next[:, None, None],
        second_next[:, None, None],
        group_codes[:, :, None],
        group_scales[:, :, None],
    )


def solution(mesh):
    return jax.shard_map(
        local,
        mesh=mesh,
        in_specs=(
            P("outer", "inner", None, None, None, None),
            P("outer", "inner", None, None, None, None),
            P(None, "inner", "outer", None, None),
            P(None, "inner", "outer", None, None),
            P(None, "inner", "outer", None, None),
        ),
        out_specs=(
            P(None, "inner", "outer", None, None),
            P(None, "inner", "outer", None, None),
            P(None, "inner", "outer", None, None),
            P(None, None, "outer", None, None),
            P(None, None, "outer", None),
        ),
        check_vma=False,
    )
```

```python
import jax
import jax.numpy as jnp
from jax import lax
from jax.sharding import Mesh
from jax.sharding import PartitionSpec as P

EPSILON = 1e-06
CODE_RANGE = 448.0
BETA_ONE = 0.9
BETA_TWO = 0.95
LEARN_RATE = 0.01
WEIGHT_DECAY = 0.1
ADAM_EPSILON = 1e-08
steps_done = 10.0


def quantize(values):
    block_scale = ((jnp.max(jnp.abs(values), axis=-1) + EPSILON) / CODE_RANGE).astype(jnp.bfloat16)
    quant_codes = (values / block_scale.astype(jnp.float32)[..., None]).astype(jnp.bfloat16)
    return (quant_codes, block_scale)


def adamw(reduced, params, first, second):
    first_next = BETA_ONE * first + (1.0 - BETA_ONE) * reduced
    second_next = BETA_TWO * second + (1.0 - BETA_TWO) * reduced * reduced
    first_hat = first_next / (1.0 - BETA_ONE**steps_done)
    second_hat = second_next / (1.0 - BETA_TWO**steps_done)
    params_next = params - LEARN_RATE * (
        first_hat / (jnp.sqrt(second_hat) + ADAM_EPSILON) + WEIGHT_DECAY * params
    )
    return (params_next, first_next, second_next)


INNER = ("x", "y_far", "y_near")
OUTER = ("z_far", "z_near", "core")


def exchange(pieces, axes):
    return lax.all_to_all(pieces, axes, 0, 0, tiled=True).astype(jnp.float32)


def local(grad_first, grad_second, master, first_moment, second_moment):
    inner, outer, rows, width = grad_first.shape[2:]
    x, y_far, y_near = (lax.axis_size(name) for name in INNER)
    z_far, z_near, core = (lax.axis_size(name) for name in OUTER)
    grads = jnp.stack([grad_first[0, 0], grad_second[0, 0]])
    grads = grads.reshape(2, x, y_far, y_near, z_far, z_near, core, rows, width)
    pieces = grads.transpose(6, 1, 5, 2, 3, 4, 0, 7, 8).reshape(core, -1, width)
    pair = jnp.sum(exchange(pieces, "core"), axis=0).astype(jnp.bfloat16)
    cross = exchange(pair.reshape(x * z_near, -1, width), ("x", "z_near"))
    cross = jnp.sum(cross, axis=0).astype(jnp.bfloat16)
    last = exchange(
        cross.reshape(y_far * y_near * z_far, 2 * rows, width), ("y_far", "y_near", "z_far")
    )
    reduced = jnp.sum(last, axis=0).reshape(2, rows, width)
    params_next, first_next, second_next = adamw(
        reduced, master[:, 0, 0], first_moment[:, 0, 0], second_moment[:, 0, 0]
    )
    weight_code, weight_scale = quantize(params_next)
    scale_row = jnp.pad(weight_scale.reshape(1, 2 * rows), ((0, 0), (0, width - 2 * rows)))
    packed = jnp.concatenate([weight_code.reshape(2 * rows, width), scale_row], axis=0)
    spread = jnp.broadcast_to(packed[None], (inner,) + packed.shape)
    group = lax.all_to_all(spread, INNER, 0, 0, tiled=True)
    group_codes = group[:, : 2 * rows].reshape(inner, 2, rows, width).transpose(1, 0, 2, 3)
    group_scales = group[:, 2 * rows, : 2 * rows].reshape(inner, 2, rows).transpose(1, 0, 2)
    return (
        params_next[:, None, None],
        first_next[:, None, None],
        second_next[:, None, None],
        group_codes[:, :, None],
        group_scales[:, :, None],
    )


def solution(mesh):
    inner, outer = mesh.devices.shape
    split = Mesh(
        mesh.devices.reshape(inner // 8, 4, 2, outer // 4, 2, 2),
        INNER + OUTER,
    )
    return jax.shard_map(
        local,
        mesh=split,
        in_specs=(P(OUTER, INNER), P(OUTER, INNER)) + (P(None, INNER, OUTER),) * 3,
        out_specs=(P(None, INNER, OUTER),) * 3 + (P(None, None, OUTER),) * 2,
        check_vma=False,
    )
```

```python
import functools

import jax
import jax.numpy as jnp
from jax import lax
from jax.experimental import pallas as pl
from jax.experimental.pallas import tpu as pltpu
from jax.sharding import Mesh
from jax.sharding import PartitionSpec as P

EPSILON = 1e-06
CODE_RANGE = 448.0
BETA_ONE = 0.9
BETA_TWO = 0.95
LEARN_RATE = 0.01
WEIGHT_DECAY = 0.1
ADAM_EPSILON = 1e-08
steps_done = 10.0


def quantize(values):
    block_scale = ((jnp.max(jnp.abs(values), axis=-1) + EPSILON) / CODE_RANGE).astype(jnp.bfloat16)
    quant_codes = (values / block_scale.astype(jnp.float32)[..., None]).astype(jnp.bfloat16)
    return (quant_codes, block_scale)


def adamw(reduced, params, first, second):
    first_next = BETA_ONE * first + (1.0 - BETA_ONE) * reduced
    second_next = BETA_TWO * second + (1.0 - BETA_TWO) * reduced * reduced
    first_hat = first_next / (1.0 - BETA_ONE**steps_done)
    second_hat = second_next / (1.0 - BETA_TWO**steps_done)
    params_next = params - LEARN_RATE * (
        first_hat / (jnp.sqrt(second_hat) + ADAM_EPSILON) + WEIGHT_DECAY * params
    )
    return (params_next, first_next, second_next)


INNER = ("x", "y_far", "y_near")
OUTER = ("z_far", "z_near", "core")


def exchange(pieces, axes):
    return lax.all_to_all(pieces, axes, 0, 0, tiled=True).astype(jnp.float32)


def sort_kernel(split, core_ref, first_ref, second_ref, keep_ref, send_ref, held, kept, sent, in_sem, out_sem):
    x, z_far, z_near = split
    inner, rows, outer, width = first_ref.shape
    span = inner // x
    half = rows * outer
    quarter = half // 2

    def load(i, k):
        part = pl.ds(i * span, span)
        return pltpu.make_async_copy(
            (first_ref, second_ref)[k].at[part], held.at[k, part], in_sem.at[i, k]
        )

    def store(i, k):
        return pltpu.make_async_copy(
            (kept, sent)[k].at[i], (keep_ref, send_ref)[k].at[i], out_sem.at[i, k]
        )

    for i in range(x):
        for k in range(2):
            load(i, k).start()
    to = lax.broadcasted_iota(jnp.int32, (2 * half, 2 * half), 0)
    at = lax.broadcasted_iota(jnp.int32, (2 * half, 2 * half), 1)
    core, near = at & 1, (at >> 1) & (z_near - 1)
    far, block = (at >> 2) & (z_far - 1), at >> 4
    place = (core ^ core_ref[0]) * half + near * quarter + far * (2 * rows) + block
    sort = jnp.where(to == place, 1.0, 0.0).astype(jnp.bfloat16)
    for i in range(x):
        for k in range(2):
            load(i, k).wait()
        for a in range(0, span, 2):
            pair = [
                jnp.concatenate(
                    [held[k, i * span + a + n].reshape(half, width) for k in range(2)], axis=0
                )
                for n in range(2)
            ]
            out = jnp.dot(
                sort, jnp.concatenate(pair, axis=1), preferred_element_type=jnp.float32
            ).astype(jnp.bfloat16)
            for n in range(2):
                for z in range(z_near):
                    lanes = slice(n * width, (n + 1) * width)
                    kept[i, z, a + n] = out[z * quarter : (z + 1) * quarter, lanes]
                    sent[i, z, a + n] = out[half + z * quarter : half + (z + 1) * quarter, lanes]
        for k in range(2):
            store(i, k).start()
    for i in range(x):
        for k in range(2):
            store(i, k).wait()


def sort_rows(core, first, second, split):
    x, z_far, z_near = split
    inner, rows, outer, width = first.shape
    shape = (x, z_near, inner // x, rows * outer // z_near, width)
    result = jax.ShapeDtypeStruct(shape, first.dtype)
    anywhere = pl.BlockSpec(memory_space=pl.ANY)
    return pl.pallas_call(
        functools.partial(sort_kernel, split),
        out_shape=(result, result),
        in_specs=[pl.BlockSpec(memory_space=pltpu.SMEM), anywhere, anywhere],
        out_specs=(anywhere, anywhere),
        scratch_shapes=[
            pltpu.VMEM((2,) + first.shape, first.dtype),
            pltpu.VMEM(shape, first.dtype),
            pltpu.VMEM(shape, first.dtype),
            pltpu.SemaphoreType.DMA((x, 2)),
            pltpu.SemaphoreType.DMA((x, 2)),
        ],
        compiler_params=pltpu.CompilerParams(vmem_limit_bytes=60 * 2**20),
    )(core, first, second)


def local(grad_first, grad_second, master, first_moment, second_moment):
    inner, outer, rows, width = grad_first.shape[2:]
    x, y_far, y_near = (lax.axis_size(name) for name in INNER)
    z_far, z_near, _ = (lax.axis_size(name) for name in OUTER)
    keep, send = sort_rows(
        lax.axis_index("core")[None],
        grad_first[0, 0].transpose(0, 2, 1, 3),
        grad_second[0, 0].transpose(0, 2, 1, 3),
        (x, z_far, z_near),
    )
    other = lax.ppermute(send, "core", [(0, 1), (1, 0)])
    pair = (keep.astype(jnp.float32) + other.astype(jnp.float32)).astype(jnp.bfloat16)
    cross = exchange(pair.reshape(x * z_near, -1, width), ("x", "z_near"))
    cross = jnp.sum(cross, axis=0).astype(jnp.bfloat16)
    last = exchange(
        cross.reshape(y_far * y_near * z_far, 2 * rows, width), ("y_far", "y_near", "z_far")
    )
    reduced = jnp.sum(last, axis=0).reshape(2, rows, width)
    params_next, first_next, second_next = adamw(
        reduced, master[:, 0, 0], first_moment[:, 0, 0], second_moment[:, 0, 0]
    )
    weight_code, weight_scale = quantize(params_next)
    scale_row = jnp.pad(weight_scale.reshape(1, 2 * rows), ((0, 0), (0, width - 2 * rows)))
    packed = jnp.concatenate([weight_code.reshape(2 * rows, width), scale_row], axis=0)
    spread = jnp.broadcast_to(packed[None], (inner,) + packed.shape)
    group = lax.all_to_all(spread, INNER, 0, 0, tiled=True)
    group_codes = group[:, : 2 * rows].reshape(inner, 2, rows, width).transpose(1, 0, 2, 3)
    group_scales = group[:, 2 * rows, : 2 * rows].reshape(inner, 2, rows).transpose(1, 0, 2)
    return (
        params_next[:, None, None],
        first_next[:, None, None],
        second_next[:, None, None],
        group_codes[:, :, None],
        group_scales[:, :, None],
    )


def solution(mesh):
    inner, outer = mesh.devices.shape
    split = Mesh(
        mesh.devices.reshape(inner // 8, 4, 2, outer // 4, 2, 2),
        INNER + OUTER,
    )
    return jax.shard_map(
        local,
        mesh=split,
        in_specs=(P(OUTER, INNER), P(OUTER, INNER)) + (P(None, INNER, OUTER),) * 3,
        out_specs=(P(None, INNER, OUTER),) * 3 + (P(None, None, OUTER),) * 2,
        check_vma=False,
    )
```

```python
import jax
import jax.numpy as jnp
from jax import lax
from jax.experimental import pallas as pl
from jax.experimental.pallas import tpu as pltpu
from jax.sharding import Mesh
from jax.sharding import PartitionSpec as P

EPSILON = 1e-06
CODE_RANGE = 448.0
BETA_ONE = 0.9
BETA_TWO = 0.95
LEARN_RATE = 0.01
WEIGHT_DECAY = 0.1
ADAM_EPSILON = 1e-08
steps_done = 10.0

INNER = ("x", "y_far", "y_near")
OUTER = ("z_far", "z_near", "core")
Z_FAR, Z_NEAR, OUTERS = 4, 2, 16
PACKED = 16
ANYWHERE = pl.BlockSpec(memory_space=pl.ANY)
SCALAR = pl.BlockSpec(memory_space=pltpu.SMEM)
VECTOR = pl.BlockSpec(memory_space=pltpu.VMEM)
f32, bf16 = jnp.float32, jnp.bfloat16


def adamw(reduced, params, first, second):
    first_next = BETA_ONE * first + (1.0 - BETA_ONE) * reduced
    second_next = BETA_TWO * second + (1.0 - BETA_TWO) * reduced * reduced
    first_hat = first_next / (1.0 - BETA_ONE**steps_done)
    second_hat = second_next / (1.0 - BETA_TWO**steps_done)
    params_next = params - LEARN_RATE * (
        first_hat / (jnp.sqrt(second_hat) + ADAM_EPSILON) + WEIGHT_DECAY * params
    )
    return (params_next, first_next, second_next)


def sorter(core, rows):
    half = rows * OUTERS
    to = lax.broadcasted_iota(jnp.int32, (half, 2 * half), 0)
    at = lax.broadcasted_iota(jnp.int32, (half, 2 * half), 1)
    near, far, block = (at >> 1) & (Z_NEAR - 1), (at >> 2) & (Z_FAR - 1), at >> 4
    place = near * (half // Z_NEAR) + far * (2 * rows) + block
    return jnp.where((to == place) & ((at & 1) == core), 1.0, 0.0).astype(bf16)


def sort_two(sort, first, second, a):
    half, width = first.shape[1] * first.shape[2], first.shape[3]
    columns = [
        jnp.concatenate([ref[a + n].reshape(half, width) for ref in (first, second)], axis=0)
        for n in range(2)
    ]
    return jnp.dot(sort, jnp.concatenate(columns, axis=1), preferred_element_type=f32)


def places(values, a, per_x, width):
    part = values.shape[0] // Z_NEAR
    for n in range(2):
        for z in range(Z_NEAR):
            yield (
                ((a + n) // per_x, z, (a + n) % per_x),
                values[z * part : (z + 1) * part, n * width : (n + 1) * width],
            )


def send_kernel(core_ref, first_ref, second_ref, send_ref, first, second, sent, in_sem, out_sem):
    inner, rows, _, width = first_ref.shape
    x, _, per_x, _, _ = send_ref.shape
    loads = in_sem.shape[0]
    span = inner // loads

    def load(i, k):
        part = pl.ds(i * span, span)
        return pltpu.make_async_copy(
            (first_ref, second_ref)[k].at[part], (first, second)[k].at[part], in_sem.at[i, k]
        )

    def store(i):
        return pltpu.make_async_copy(sent.at[i], send_ref.at[i], out_sem.at[i])

    for i in range(loads):
        for k in range(2):
            load(i, k).start()
    sort = sorter(1 - core_ref[0], rows)
    for a in range(0, inner, 2):
        if a % span == 0:
            for k in range(2):
                load(a // span, k).wait()
        values = sort_two(sort, first, second, a).astype(bf16)
        for place, piece in places(values, a, per_x, width):
            sent[place] = piece
        if (a + 2) % per_x == 0:
            store(a // per_x).start()
    for i in range(x):
        store(i).wait()


def rows_to_send(core, first, second, x):
    inner, rows, outer, width = first.shape
    shape = (x, Z_NEAR, inner // x, rows * outer // 2, width)
    return pl.pallas_call(
        send_kernel,
        out_shape=jax.ShapeDtypeStruct(shape, bf16),
        in_specs=[SCALAR, ANYWHERE, ANYWHERE],
        out_specs=ANYWHERE,
        scratch_shapes=[
            pltpu.VMEM(first.shape, bf16),
            pltpu.VMEM(first.shape, bf16),
            pltpu.VMEM(shape, bf16),
            pltpu.SemaphoreType.DMA((2, 2)),
            pltpu.SemaphoreType.DMA((x,)),
        ],
        compiler_params=pltpu.CompilerParams(vmem_limit_bytes=60 * 2**20),
    )(core, first, second)


def add_kernel(core_ref, first_ref, second_ref, other_ref, out_ref):
    inner, rows, _, width = first_ref.shape
    per_x = other_ref.shape[2]
    sort = sorter(core_ref[0], rows)
    for a in range(0, inner, 2):
        values = sort_two(sort, first_ref, second_ref, a)
        for place, piece in places(values, a, per_x, width):
            out_ref[place] = (piece + other_ref[place].astype(f32)).astype(bf16)


def add_own_rows(core, first, second, other):
    return pl.pallas_call(
        add_kernel,
        out_shape=jax.ShapeDtypeStruct(other.shape, bf16),
        in_specs=[SCALAR, VECTOR, VECTOR, VECTOR],
        out_specs=VECTOR,
        compiler_params=pltpu.CompilerParams(vmem_limit_bytes=16 * 2**20),
    )(core, first, second, other)


def fold_kernel(terms_ref, out_ref):
    total = jnp.sum(terms_ref[...].astype(f32), axis=0)
    pieces, rows, _ = out_ref.shape
    for i in range(pieces):
        out_ref[i] = total[i * rows : (i + 1) * rows].astype(bf16)


def fold(terms, shape):
    return pl.pallas_call(
        fold_kernel,
        out_shape=jax.ShapeDtypeStruct(shape, bf16),
        in_specs=[VECTOR],
        out_specs=VECTOR,
        compiler_params=pltpu.CompilerParams(vmem_limit_bytes=8 * 2**20),
    )(terms)


def update_kernel(terms_ref, master_ref, first_ref, second_ref, *out_refs):
    _, blocks, width = terms_ref.shape
    reduced = jnp.sum(terms_ref[...].astype(f32), axis=0)
    state = (
        jnp.concatenate([ref[k] for k in range(blocks)], axis=0)
        for ref in (master_ref, first_ref, second_ref)
    )
    updated = adamw(reduced, *state)
    for ref, value in zip(out_refs, updated):
        for k in range(blocks):
            ref[k] = value[k : k + 1]
    params_next = updated[0]
    largest = jnp.max(jnp.abs(params_next), axis=-1, keepdims=True)
    scale = ((largest + EPSILON) / CODE_RANGE).astype(bf16).astype(f32)
    row = lax.broadcasted_iota(jnp.int32, (blocks, width), 0)
    lane = lax.broadcasted_iota(jnp.int32, (blocks, width), 1)
    scale_row = jnp.sum(jnp.where(row == lane, scale, 0.0), axis=0, keepdims=True)
    filling = jnp.zeros((PACKED - blocks - 1, width), f32)
    packed = jnp.concatenate([params_next / scale, scale_row, filling], axis=0).astype(bf16)
    spread_ref = out_refs[3]
    for i in range(spread_ref.shape[0]):
        spread_ref[i] = packed


def update(terms, master, first, second, members):
    state = jax.ShapeDtypeStruct(master.shape, f32)
    spread = jax.ShapeDtypeStruct((members, PACKED, master.shape[-1]), bf16)
    return pl.pallas_call(
        update_kernel,
        out_shape=(state, state, state, spread),
        in_specs=[VECTOR] * 4,
        out_specs=(VECTOR,) * 4,
        compiler_params=pltpu.CompilerParams(vmem_limit_bytes=8 * 2**20),
    )(terms, master, first, second)


def unpack_kernel(group_ref, codes_ref, scales_ref):
    members, packed, width = group_ref.shape
    blocks = codes_ref.shape[0]
    shape = ((blocks + 1) * members, members * packed)
    to = lax.broadcasted_iota(jnp.int32, shape, 0)
    at = lax.broadcasted_iota(jnp.int32, shape, 1)
    sort = jnp.where(to == (at & (PACKED - 1)) * members + (at >> 4), 1.0, 0.0).astype(bf16)
    rows = jnp.dot(sort, group_ref[...].reshape(members * packed, width), preferred_element_type=f32)
    for k in range(blocks):
        codes_ref[k] = rows[k * members : (k + 1) * members].astype(bf16)
    scales = rows[blocks * members :].T
    half = blocks // 2
    for j in range(half):
        scales_ref[j] = jnp.concatenate(
            [scales[k : k + 1] for k in (j, half + j)], axis=0
        ).astype(bf16)


def unpack(group, blocks):
    members, _, width = group.shape
    return pl.pallas_call(
        unpack_kernel,
        out_shape=(
            jax.ShapeDtypeStruct((blocks, members, width), bf16),
            jax.ShapeDtypeStruct((blocks // 2, 2, members), bf16),
        ),
        in_specs=[VECTOR],
        out_specs=(VECTOR, VECTOR),
        compiler_params=pltpu.CompilerParams(vmem_limit_bytes=8 * 2**20),
    )(group)


def exchange(pieces, axes):
    return lax.all_to_all(pieces, axes, 0, 0, tiled=True)


def local(grad_first, grad_second, master, first_moment, second_moment):
    inner, _, rows, width = grad_first.shape[2:]
    blocks = 2 * rows
    x = lax.axis_size("x")
    core = lax.axis_index("core")[None]
    grads = [g[0, 0].transpose(0, 2, 1, 3) for g in (grad_first, grad_second)]
    other = lax.ppermute(rows_to_send(core, *grads, x), "core", [(0, 1), (1, 0)])
    pair = add_own_rows(core, *grads, other)
    cross = exchange(pair.reshape(x * Z_NEAR, -1, width), ("x", "z_near"))
    cross = fold(cross, (inner // x * Z_FAR, blocks, width))
    last = exchange(cross, ("y_far", "y_near", "z_far"))
    state = [v.reshape(blocks, 1, width) for v in (master, first_moment, second_moment)]
    *updated, spread = update(last, *state, inner)
    codes, scales = unpack(exchange(spread, INNER), blocks)
    codes = codes.reshape(2, rows, inner, width).transpose(0, 2, 1, 3)
    return (
        *(v.reshape(master.shape) for v in updated),
        codes[:, :, None],
        scales.transpose(1, 2, 0)[:, :, None],
    )


def solution(mesh):
    inner, outer = mesh.devices.shape
    split = Mesh(
        mesh.devices.reshape(inner // 8, 4, 2, outer // 4, Z_NEAR, 2),
        INNER + OUTER,
    )
    return jax.shard_map(
        local,
        mesh=split,
        in_specs=(P(OUTER, INNER), P(OUTER, INNER)) + (P(None, INNER, OUTER),) * 3,
        out_specs=(P(None, INNER, OUTER),) * 3 + (P(None, None, OUTER),) * 2,
        check_vma=False,
    )
```

```python
import jax
import jax.numpy as jnp
from jax import lax
from jax.experimental import pallas as pl
from jax.experimental.pallas import tpu as pltpu
from jax.sharding import Mesh
from jax.sharding import PartitionSpec as P

EPSILON = 1e-06
CODE_RANGE = 448.0
BETA_ONE = 0.9
BETA_TWO = 0.95
LEARN_RATE = 0.01
WEIGHT_DECAY = 0.1
ADAM_EPSILON = 1e-08
steps_done = 10.0

INNER = ("x", "y_far", "y_near")
OUTER = ("z_far", "z_near", "core")
Z_FAR, Z_NEAR, OUTERS = 4, 2, 16
PACKED = 16
ANYWHERE = pl.BlockSpec(memory_space=pl.ANY)
SCALAR = pl.BlockSpec(memory_space=pltpu.SMEM)
VECTOR = pl.BlockSpec(memory_space=pltpu.VMEM)
f32, bf16 = jnp.float32, jnp.bfloat16


def adamw(reduced, params, first, second):
    first_next = BETA_ONE * first + (1.0 - BETA_ONE) * reduced
    second_next = BETA_TWO * second + (1.0 - BETA_TWO) * reduced * reduced
    first_hat = first_next / (1.0 - BETA_ONE**steps_done)
    second_hat = second_next / (1.0 - BETA_TWO**steps_done)
    params_next = params - LEARN_RATE * (
        first_hat / (jnp.sqrt(second_hat) + ADAM_EPSILON) + WEIGHT_DECAY * params
    )
    return (params_next, first_next, second_next)


def sorter(core, rows):
    half = rows * OUTERS
    to = lax.broadcasted_iota(jnp.int32, (half, 2 * half), 0)
    at = lax.broadcasted_iota(jnp.int32, (half, 2 * half), 1)
    near, far, block = (at >> 1) & (Z_NEAR - 1), (at >> 2) & (Z_FAR - 1), at >> 4
    place = near * (half // Z_NEAR) + far * (2 * rows) + block
    return jnp.where((to == place) & ((at & 1) == core), 1.0, 0.0).astype(bf16)


def sort_two(sort, first, second, a):
    half, width = first.shape[1] * first.shape[2], first.shape[3]
    columns = [
        jnp.concatenate([ref[a + n].reshape(half, width) for ref in (first, second)], axis=0)
        for n in range(2)
    ]
    return jnp.dot(sort, jnp.concatenate(columns, axis=1), preferred_element_type=f32)


def places(values, a, per_x, width):
    part = values.shape[0] // Z_NEAR
    for n in range(2):
        for z in range(Z_NEAR):
            yield (
                ((a + n) // per_x, z, (a + n) % per_x),
                values[z * part : (z + 1) * part, n * width : (n + 1) * width],
            )


def send_kernel(core_ref, first_ref, second_ref, send_ref, first, second, sem):
    inner, rows, _, width = first_ref.shape
    per_x = send_ref.shape[2]
    loads = sem.shape[0]
    span = inner // loads

    def load(i, k):
        part = pl.ds(i * span, span)
        return pltpu.make_async_copy(
            (first_ref, second_ref)[k].at[part], (first, second)[k].at[part], sem.at[i, k]
        )

    for i in range(loads):
        for k in range(2):
            load(i, k).start()
    sort = sorter(1 - core_ref[0], rows)
    for a in range(0, inner, 2):
        if a % span == 0:
            for k in range(2):
                load(a // span, k).wait()
        values = sort_two(sort, first, second, a).astype(bf16)
        for place, piece in places(values, a, per_x, width):
            send_ref[place] = piece


def rows_to_send(core, first, second, x):
    inner, rows, outer, width = first.shape
    shape = (x, Z_NEAR, inner // x, rows * outer // 2, width)
    return pl.pallas_call(
        send_kernel,
        out_shape=jax.ShapeDtypeStruct(shape, bf16),
        in_specs=[SCALAR, ANYWHERE, ANYWHERE],
        out_specs=VECTOR,
        scratch_shapes=[
            pltpu.VMEM(first.shape, bf16),
            pltpu.VMEM(first.shape, bf16),
            pltpu.SemaphoreType.DMA((2, 2)),
        ],
        compiler_params=pltpu.CompilerParams(vmem_limit_bytes=16 * 2**20),
    )(core, *(pltpu.with_memory_space_constraint(g, pltpu.HBM) for g in (first, second)))


def add_kernel(core_ref, first_ref, second_ref, other_ref, out_ref):
    inner, rows, _, width = first_ref.shape
    per_x = other_ref.shape[2]
    sort = sorter(core_ref[0], rows)
    for a in range(0, inner, 2):
        values = sort_two(sort, first_ref, second_ref, a)
        for place, piece in places(values, a, per_x, width):
            out_ref[place] = (piece + other_ref[place].astype(f32)).astype(bf16)


def add_own_rows(core, first, second, other):
    return pl.pallas_call(
        add_kernel,
        out_shape=jax.ShapeDtypeStruct(other.shape, bf16),
        in_specs=[SCALAR, VECTOR, VECTOR, VECTOR],
        out_specs=VECTOR,
        compiler_params=pltpu.CompilerParams(vmem_limit_bytes=16 * 2**20),
    )(core, first, second, other)


def fold_kernel(terms_ref, out_ref):
    total = jnp.sum(terms_ref[...].astype(f32), axis=0)
    pieces, rows, _ = out_ref.shape
    for i in range(pieces):
        out_ref[i] = total[i * rows : (i + 1) * rows].astype(bf16)


def fold(terms, shape):
    return pl.pallas_call(
        fold_kernel,
        out_shape=jax.ShapeDtypeStruct(shape, bf16),
        in_specs=[VECTOR],
        out_specs=VECTOR,
        compiler_params=pltpu.CompilerParams(vmem_limit_bytes=8 * 2**20),
    )(terms)


def update_kernel(terms_ref, master_ref, first_ref, second_ref, *out_refs):
    _, blocks, width = terms_ref.shape
    reduced = jnp.sum(terms_ref[...].astype(f32), axis=0)
    state = (
        jnp.concatenate([ref[k] for k in range(blocks)], axis=0)
        for ref in (master_ref, first_ref, second_ref)
    )
    updated = adamw(reduced, *state)
    for ref, value in zip(out_refs, updated):
        for k in range(blocks):
            ref[k] = value[k : k + 1]
    params_next = updated[0]
    largest = jnp.max(jnp.abs(params_next), axis=-1, keepdims=True)
    scale = ((largest + EPSILON) / CODE_RANGE).astype(bf16).astype(f32)
    row = lax.broadcasted_iota(jnp.int32, (blocks, width), 0)
    lane = lax.broadcasted_iota(jnp.int32, (blocks, width), 1)
    scale_row = jnp.sum(jnp.where(row == lane, scale, 0.0), axis=0, keepdims=True)
    filling = jnp.zeros((PACKED - blocks - 1, width), f32)
    packed = jnp.concatenate([params_next / scale, scale_row, filling], axis=0).astype(bf16)
    spread_ref = out_refs[3]
    for i in range(spread_ref.shape[0]):
        spread_ref[i] = packed


def update(terms, master, first, second, members):
    state = jax.ShapeDtypeStruct(master.shape, f32)
    spread = jax.ShapeDtypeStruct((members, PACKED, master.shape[-1]), bf16)
    return pl.pallas_call(
        update_kernel,
        out_shape=(state, state, state, spread),
        in_specs=[VECTOR] * 4,
        out_specs=(VECTOR,) * 4,
        compiler_params=pltpu.CompilerParams(vmem_limit_bytes=8 * 2**20),
    )(terms, master, first, second)


def unpack_kernel(group_ref, codes_ref, scales_ref, wide):
    members, packed, width = group_ref.shape
    blocks = codes_ref.shape[0]
    wide[...] = group_ref[...].astype(f32).reshape(members * packed, width)

    def row(k):
        return wide[pl.ds(k, members, stride=packed), :]

    for k in range(blocks):
        codes_ref[k] = row(k).astype(bf16)
    scales = row(blocks).T
    half = blocks // 2
    for j in range(half):
        scales_ref[j] = jnp.concatenate(
            [scales[k : k + 1] for k in (j, half + j)], axis=0
        ).astype(bf16)


def unpack(group, blocks):
    members, packed, width = group.shape
    return pl.pallas_call(
        unpack_kernel,
        out_shape=(
            jax.ShapeDtypeStruct((blocks, members, width), bf16),
            jax.ShapeDtypeStruct((blocks // 2, 2, members), bf16),
        ),
        in_specs=[VECTOR],
        out_specs=(VECTOR, VECTOR),
        scratch_shapes=[pltpu.VMEM((members * packed, width), f32)],
        compiler_params=pltpu.CompilerParams(vmem_limit_bytes=8 * 2**20),
    )(group)


def exchange(pieces, axes):
    return lax.all_to_all(pieces, axes, 0, 0, tiled=True)


def local(grad_first, grad_second, master, first_moment, second_moment):
    inner, _, rows, width = grad_first.shape[2:]
    blocks = 2 * rows
    x = lax.axis_size("x")
    core = lax.axis_index("core")[None]
    grads = [g[0, 0].transpose(0, 2, 1, 3) for g in (grad_first, grad_second)]
    other = lax.ppermute(rows_to_send(core, *grads, x), "core", [(0, 1), (1, 0)])
    pair = add_own_rows(core, *grads, other)
    cross = exchange(pair.reshape(x * Z_NEAR, -1, width), ("x", "z_near"))
    cross = fold(cross, (inner // x * Z_FAR, blocks, width))
    last = exchange(cross, ("y_far", "y_near", "z_far"))
    state = [v.reshape(blocks, 1, width) for v in (master, first_moment, second_moment)]
    *updated, spread = update(last, *state, inner)
    codes, scales = unpack(exchange(spread, INNER), blocks)
    codes = codes.reshape(2, rows, inner, width).transpose(0, 2, 1, 3)
    return (
        *(v.reshape(master.shape) for v in updated),
        codes[:, :, None],
        scales.transpose(1, 2, 0)[:, :, None],
    )


def solution(mesh):
    inner, outer = mesh.devices.shape
    split = Mesh(
        mesh.devices.reshape(inner // 8, 4, 2, outer // 4, Z_NEAR, 2),
        INNER + OUTER,
    )
    return jax.shard_map(
        local,
        mesh=split,
        in_specs=(P(OUTER, INNER), P(OUTER, INNER)) + (P(None, INNER, OUTER),) * 3,
        out_specs=(P(None, INNER, OUTER),) * 3 + (P(None, None, OUTER),) * 2,
        check_vma=False,
    )
```

```python
import jax
import jax.numpy as jnp
from jax import lax
from jax.experimental import pallas as pl
from jax.experimental.pallas import tpu as pltpu
from jax.sharding import Mesh
from jax.sharding import PartitionSpec as P

EPSILON = 1e-06
CODE_RANGE = 448.0
BETA_ONE = 0.9
BETA_TWO = 0.95
LEARN_RATE = 0.01
WEIGHT_DECAY = 0.1
ADAM_EPSILON = 1e-08
steps_done = 10.0

INNER = ("x", "y_far", "y_near")
OUTER = ("z_far", "z_near", "core")
Z_FAR, Z_NEAR, OUTERS = 4, 2, 16
PACKED = 16
ANYWHERE = pl.BlockSpec(memory_space=pl.ANY)
SCALAR = pl.BlockSpec(memory_space=pltpu.SMEM)
VECTOR = pl.BlockSpec(memory_space=pltpu.VMEM)
f32, bf16 = jnp.float32, jnp.bfloat16


def adamw(reduced, params, first, second):
    first_next = BETA_ONE * first + (1.0 - BETA_ONE) * reduced
    second_next = BETA_TWO * second + (1.0 - BETA_TWO) * reduced * reduced
    first_hat = first_next / (1.0 - BETA_ONE**steps_done)
    second_hat = second_next / (1.0 - BETA_TWO**steps_done)
    params_next = params - LEARN_RATE * (
        first_hat / (jnp.sqrt(second_hat) + ADAM_EPSILON) + WEIGHT_DECAY * params
    )
    return (params_next, first_next, second_next)


def sorter(core, rows):
    half = rows * OUTERS
    to = lax.broadcasted_iota(jnp.int32, (half, 2 * half), 0)
    at = lax.broadcasted_iota(jnp.int32, (half, 2 * half), 1)
    near, far, block = (at >> 1) & (Z_NEAR - 1), (at >> 2) & (Z_FAR - 1), at >> 4
    place = near * (half // Z_NEAR) + far * (2 * rows) + block
    return jnp.where((to == place) & ((at & 1) == core), 1.0, 0.0).astype(bf16)


def sort_two(sort, first, second, a):
    half, width = first.shape[1] * first.shape[2], first.shape[3]
    columns = [
        jnp.concatenate([ref[a + n].reshape(half, width) for ref in (first, second)], axis=0)
        for n in range(2)
    ]
    return jnp.dot(sort, jnp.concatenate(columns, axis=1), preferred_element_type=f32)


def places(values, a, y_far, width):
    part = values.shape[0] // Z_NEAR
    for n in range(2):
        for z in range(Z_NEAR):
            yield (
                (a // (2 * y_far), n, z, a // 2 % y_far),
                values[z * part : (z + 1) * part, n * width : (n + 1) * width],
            )


def send_kernel(core_ref, first_ref, second_ref, send_ref, first, second, sem):
    inner, rows, _, width = first_ref.shape
    y_far = send_ref.shape[3]
    loads = sem.shape[0]
    span = inner // loads

    def load(i, k):
        part = pl.ds(i * span, span)
        return pltpu.make_async_copy(
            (first_ref, second_ref)[k].at[part], (first, second)[k].at[part], sem.at[i, k]
        )

    for i in range(loads):
        for k in range(2):
            load(i, k).start()
    sort = sorter(1 - core_ref[0], rows)
    for a in range(0, inner, 2):
        if a % span == 0:
            for k in range(2):
                load(a // span, k).wait()
        values = sort_two(sort, first, second, a).astype(bf16)
        for place, piece in places(values, a, y_far, width):
            send_ref[place] = piece


def rows_to_send(core, first, second, x):
    inner, rows, outer, width = first.shape
    shape = (x, 2, Z_NEAR, inner // x // 2, rows * outer // 2, width)
    return pl.pallas_call(
        send_kernel,
        out_shape=jax.ShapeDtypeStruct(shape, bf16),
        in_specs=[SCALAR, ANYWHERE, ANYWHERE],
        out_specs=VECTOR,
        scratch_shapes=[
            pltpu.VMEM(first.shape, bf16),
            pltpu.VMEM(first.shape, bf16),
            pltpu.SemaphoreType.DMA((2, 2)),
        ],
        compiler_params=pltpu.CompilerParams(vmem_limit_bytes=16 * 2**20),
    )(core, *(pltpu.with_memory_space_constraint(g, pltpu.HBM) for g in (first, second)))


def add_kernel(core_ref, first_ref, second_ref, other_ref, out_ref):
    inner, rows, _, width = first_ref.shape
    y_far = other_ref.shape[3]
    sort = sorter(core_ref[0], rows)
    for a in range(0, inner, 2):
        values = sort_two(sort, first_ref, second_ref, a)
        for place, piece in places(values, a, y_far, width):
            out_ref[place] = (piece + other_ref[place].astype(f32)).astype(bf16)


def add_own_rows(core, first, second, other):
    return pl.pallas_call(
        add_kernel,
        out_shape=jax.ShapeDtypeStruct(other.shape, bf16),
        in_specs=[SCALAR, VECTOR, VECTOR, VECTOR],
        out_specs=VECTOR,
        compiler_params=pltpu.CompilerParams(vmem_limit_bytes=16 * 2**20),
    )(core, first, second, other)


def fold_kernel(terms_ref, out_ref):
    total = jnp.sum(terms_ref[...].astype(f32), axis=0)
    pieces, rows, _ = out_ref.shape
    for i in range(pieces):
        out_ref[i] = total[i * rows : (i + 1) * rows].astype(bf16)


def fold(terms, shape):
    return pl.pallas_call(
        fold_kernel,
        out_shape=jax.ShapeDtypeStruct(shape, bf16),
        in_specs=[VECTOR],
        out_specs=VECTOR,
        compiler_params=pltpu.CompilerParams(vmem_limit_bytes=8 * 2**20),
    )(terms)


def update_kernel(terms_ref, master_ref, first_ref, second_ref, *out_refs):
    _, blocks, width = terms_ref.shape
    reduced = jnp.sum(terms_ref[...].astype(f32), axis=0)
    state = (
        jnp.concatenate([ref[k] for k in range(blocks)], axis=0)
        for ref in (master_ref, first_ref, second_ref)
    )
    updated = adamw(reduced, *state)
    for ref, value in zip(out_refs, updated):
        for k in range(blocks):
            ref[k] = value[k : k + 1]
    params_next = updated[0]
    largest = jnp.max(jnp.abs(params_next), axis=-1, keepdims=True)
    scale = ((largest + EPSILON) / CODE_RANGE).astype(bf16).astype(f32)
    row = lax.broadcasted_iota(jnp.int32, (blocks, width), 0)
    lane = lax.broadcasted_iota(jnp.int32, (blocks, width), 1)
    scale_row = jnp.sum(jnp.where(row == lane, scale, 0.0), axis=0, keepdims=True)
    filling = jnp.zeros((PACKED - blocks - 1, width), f32)
    packed = jnp.concatenate([params_next / scale, scale_row, filling], axis=0).astype(bf16)
    spread_ref = out_refs[3]
    for i in range(spread_ref.shape[0]):
        spread_ref[i] = packed


def update(terms, master, first, second, members):
    state = jax.ShapeDtypeStruct(master.shape, f32)
    spread = jax.ShapeDtypeStruct((members, PACKED, master.shape[-1]), bf16)
    return pl.pallas_call(
        update_kernel,
        out_shape=(state, state, state, spread),
        in_specs=[VECTOR] * 4,
        out_specs=(VECTOR,) * 4,
        compiler_params=pltpu.CompilerParams(vmem_limit_bytes=8 * 2**20),
    )(terms, master, first, second)


def unpack_kernel(group_ref, codes_ref, scales_ref, wide):
    members, packed, width = group_ref.shape
    blocks = codes_ref.shape[0]
    wide[...] = group_ref[...].astype(f32).reshape(members * packed, width)

    def row(k):
        return wide[pl.ds(k, members, stride=packed), :]

    for k in range(blocks):
        codes_ref[k] = row(k).astype(bf16)
    scales = row(blocks).T
    half = blocks // 2
    for j in range(half):
        scales_ref[j] = jnp.concatenate(
            [scales[k : k + 1] for k in (j, half + j)], axis=0
        ).astype(bf16)


def unpack(group, blocks):
    members, packed, width = group.shape
    return pl.pallas_call(
        unpack_kernel,
        out_shape=(
            jax.ShapeDtypeStruct((blocks, members, width), bf16),
            jax.ShapeDtypeStruct((blocks // 2, 2, members), bf16),
        ),
        in_specs=[VECTOR],
        out_specs=(VECTOR, VECTOR),
        scratch_shapes=[pltpu.VMEM((members * packed, width), f32)],
        compiler_params=pltpu.CompilerParams(vmem_limit_bytes=8 * 2**20),
    )(group)


def exchange(pieces, axes):
    return lax.all_to_all(pieces, axes, 0, 0, tiled=True)


def local(grad_first, grad_second, master, first_moment, second_moment):
    inner, _, rows, width = grad_first.shape[2:]
    blocks = 2 * rows
    x = lax.axis_size("x")
    core = lax.axis_index("core")[None]
    grads = [g[0, 0].transpose(0, 2, 1, 3) for g in (grad_first, grad_second)]
    other = lax.ppermute(rows_to_send(core, *grads, x), "core", [(0, 1), (1, 0)])
    pair = add_own_rows(core, *grads, other)
    near = exchange(pair.reshape(x * 2 * Z_NEAR, -1, width), ("x", "y_near", "z_near"))
    near = fold(near, (inner // x // 2 * Z_FAR, blocks, width))
    last = exchange(near, ("y_far", "z_far"))
    state = [v.reshape(blocks, 1, width) for v in (master, first_moment, second_moment)]
    *updated, spread = update(last, *state, inner)
    codes, scales = unpack(exchange(spread, INNER), blocks)
    codes = codes.reshape(2, rows, inner, width).transpose(0, 2, 1, 3)
    return (
        *(v.reshape(master.shape) for v in updated),
        codes[:, :, None],
        scales.transpose(1, 2, 0)[:, :, None],
    )


def solution(mesh):
    inner, outer = mesh.devices.shape
    split = Mesh(
        mesh.devices.reshape(inner // 8, 4, 2, outer // 4, Z_NEAR, 2),
        INNER + OUTER,
    )
    return jax.shard_map(
        local,
        mesh=split,
        in_specs=(P(OUTER, INNER), P(OUTER, INNER)) + (P(None, INNER, OUTER),) * 3,
        out_specs=(P(None, INNER, OUTER),) * 3 + (P(None, None, OUTER),) * 2,
        check_vma=False,
    )
```

```python
import jax
import jax.numpy as jnp
from jax import lax
from jax.experimental import pallas as pl
from jax.experimental.pallas import tpu as pltpu
from jax.sharding import Mesh
from jax.sharding import PartitionSpec as P

EPSILON = 1e-06
CODE_RANGE = 448.0
BETA_ONE = 0.9
BETA_TWO = 0.95
LEARN_RATE = 0.01
WEIGHT_DECAY = 0.1
ADAM_EPSILON = 1e-08
steps_done = 10.0

INNER = ("x", "y_far", "y_near")
OUTER = ("z_far", "z_near", "core")
Z_FAR, Z_NEAR, OUTERS = 4, 2, 16
PACKED = 16
ANYWHERE = pl.BlockSpec(memory_space=pl.ANY)
SCALAR = pl.BlockSpec(memory_space=pltpu.SMEM)
VECTOR = pl.BlockSpec(memory_space=pltpu.VMEM)
f32, bf16 = jnp.float32, jnp.bfloat16


def adamw(reduced, params, first, second):
    first_next = BETA_ONE * first + (1.0 - BETA_ONE) * reduced
    second_next = BETA_TWO * second + (1.0 - BETA_TWO) * reduced * reduced
    first_hat = first_next / (1.0 - BETA_ONE**steps_done)
    second_hat = second_next / (1.0 - BETA_TWO**steps_done)
    params_next = params - LEARN_RATE * (
        first_hat / (jnp.sqrt(second_hat) + ADAM_EPSILON) + WEIGHT_DECAY * params
    )
    return (params_next, first_next, second_next)


def sorter(core, rows):
    half = rows * OUTERS
    to = lax.broadcasted_iota(jnp.int32, (half, 2 * half), 0)
    at = lax.broadcasted_iota(jnp.int32, (half, 2 * half), 1)
    near, far, block = (at >> 1) & (Z_NEAR - 1), (at >> 2) & (Z_FAR - 1), at >> 4
    place = near * (half // Z_NEAR) + far * (2 * rows) + block
    return jnp.where((to == place) & ((at & 1) == core), 1.0, 0.0).astype(bf16)


def sort_two(sort, first, second, a):
    half, width = first.shape[1] * first.shape[2], first.shape[3]
    columns = [
        jnp.concatenate([ref[a + n].reshape(half, width) for ref in (first, second)], axis=0)
        for n in range(2)
    ]
    return jnp.dot(sort, jnp.concatenate(columns, axis=1), preferred_element_type=f32)


def places(values, a, y_far, width):
    part = values.shape[0] // Z_NEAR
    for n in range(2):
        for z in range(Z_NEAR):
            yield (
                (a // (2 * y_far), n, z, a // 2 % y_far),
                values[z * part : (z + 1) * part, n * width : (n + 1) * width],
            )


def send_kernel(core_ref, first_ref, second_ref, send_ref, first, second, sem):
    inner, rows, _, width = first_ref.shape
    y_far = send_ref.shape[3]
    loads = sem.shape[0]
    span = inner // loads

    def load(i, k):
        part = pl.ds(i * span, span)
        return pltpu.make_async_copy(
            (first_ref, second_ref)[k].at[part], (first, second)[k].at[part], sem.at[i, k]
        )

    for i in range(loads):
        for k in range(2):
            load(i, k).start()
    sort = sorter(1 - core_ref[0], rows)
    for a in range(0, inner, 2):
        if a % span == 0:
            for k in range(2):
                load(a // span, k).wait()
        values = sort_two(sort, first, second, a).astype(bf16)
        for place, piece in places(values, a, y_far, width):
            send_ref[place] = piece


def rows_to_send(core, first, second, x):
    inner, rows, outer, width = first.shape
    shape = (x, 2, Z_NEAR, inner // x // 2, rows * outer // 2, width)
    return pl.pallas_call(
        send_kernel,
        out_shape=jax.ShapeDtypeStruct(shape, bf16),
        in_specs=[SCALAR, ANYWHERE, ANYWHERE],
        out_specs=VECTOR,
        scratch_shapes=[
            pltpu.VMEM(first.shape, bf16),
            pltpu.VMEM(first.shape, bf16),
            pltpu.SemaphoreType.DMA((2, 2)),
        ],
        compiler_params=pltpu.CompilerParams(vmem_limit_bytes=16 * 2**20),
    )(core, *(pltpu.with_memory_space_constraint(g, pltpu.HBM) for g in (first, second)))


def add_kernel(core_ref, first_ref, second_ref, other_ref, out_ref):
    inner, rows, _, width = first_ref.shape
    y_far = other_ref.shape[3]
    sort = sorter(core_ref[0], rows)
    for a in range(0, inner, 2):
        values = sort_two(sort, first_ref, second_ref, a)
        for place, piece in places(values, a, y_far, width):
            out_ref[place] = (piece + other_ref[place].astype(f32)).astype(bf16)


def add_own_rows(core, first, second, other):
    return pl.pallas_call(
        add_kernel,
        out_shape=jax.ShapeDtypeStruct(other.shape, bf16),
        in_specs=[SCALAR, VECTOR, VECTOR, VECTOR],
        out_specs=VECTOR,
        compiler_params=pltpu.CompilerParams(vmem_limit_bytes=16 * 2**20),
    )(core, first, second, other)


def fold_kernel(terms_ref, out_ref):
    total = jnp.sum(terms_ref[...].astype(f32), axis=0)
    pieces, rows, _ = out_ref.shape
    for i in range(pieces):
        out_ref[i] = total[i * rows : (i + 1) * rows].astype(bf16)


def fold(terms, shape):
    return pl.pallas_call(
        fold_kernel,
        out_shape=jax.ShapeDtypeStruct(shape, bf16),
        in_specs=[VECTOR],
        out_specs=VECTOR,
        compiler_params=pltpu.CompilerParams(vmem_limit_bytes=8 * 2**20),
    )(terms)


def update_kernel(terms_ref, master_ref, first_ref, second_ref, *out_refs):
    _, blocks, width = terms_ref.shape
    reduced = jnp.sum(terms_ref[...].astype(f32), axis=0)
    state = (
        jnp.concatenate([ref[k] for k in range(blocks)], axis=0)
        for ref in (master_ref, first_ref, second_ref)
    )
    updated = adamw(reduced, *state)
    for ref, value in zip(out_refs, updated):
        for k in range(blocks):
            ref[k] = value[k : k + 1]
    params_next = updated[0]
    largest = jnp.max(jnp.abs(params_next), axis=-1, keepdims=True)
    scale = ((largest + EPSILON) / CODE_RANGE).astype(bf16).astype(f32)
    row = lax.broadcasted_iota(jnp.int32, (blocks, width), 0)
    lane = lax.broadcasted_iota(jnp.int32, (blocks, width), 1)
    scale_row = jnp.sum(jnp.where(row == lane, scale, 0.0), axis=0, keepdims=True)
    filling = jnp.zeros((PACKED - blocks - 1, width), f32)
    packed = jnp.concatenate([params_next / scale, scale_row, filling], axis=0).astype(bf16)
    spread_ref = out_refs[3]
    for i in range(spread_ref.shape[0]):
        spread_ref[i] = packed


def update(terms, master, first, second, members):
    state = pltpu.VMEM(master.shape, f32)
    spread = pltpu.VMEM((members, PACKED, master.shape[-1]), bf16)
    return pl.pallas_call(
        update_kernel,
        out_shape=(state, state, state, spread),
        in_specs=[VECTOR] * 4,
        out_specs=(VECTOR,) * 4,
        compiler_params=pltpu.CompilerParams(vmem_limit_bytes=8 * 2**20),
    )(terms, master, first, second)


def finish_kernel(group_ref, *refs):
    state_refs, (codes_ref, scales_ref), stored_refs = refs[:3], refs[3:5], refs[5:8]
    wide, sem = refs[8:]
    copies = [
        pltpu.make_async_copy(new, stored, sem.at[i])
        for i, (new, stored) in enumerate(zip(state_refs, stored_refs))
    ]
    for copy in copies:
        copy.start()
    members, packed, width = group_ref.shape
    blocks = codes_ref.shape[0]
    wide[...] = group_ref[...].astype(f32).reshape(members * packed, width)

    def row(k):
        return wide[pl.ds(k, members, stride=packed), :]

    for k in range(blocks):
        codes_ref[k] = row(k).astype(bf16)
    scales = row(blocks).T
    half = blocks // 2
    for j in range(half):
        scales_ref[j] = jnp.concatenate(
            [scales[k : k + 1] for k in (j, half + j)], axis=0
        ).astype(bf16)
    for copy in copies:
        copy.wait()


def finish(group, state):
    members, packed, width = group.shape
    blocks = state[0].shape[0]
    stored = jax.ShapeDtypeStruct(state[0].shape, f32)
    return pl.pallas_call(
        finish_kernel,
        out_shape=(
            jax.ShapeDtypeStruct((blocks, members, width), bf16),
            jax.ShapeDtypeStruct((blocks // 2, 2, members), bf16),
            stored,
            stored,
            stored,
        ),
        in_specs=[VECTOR] * 4,
        out_specs=(VECTOR, VECTOR, ANYWHERE, ANYWHERE, ANYWHERE),
        scratch_shapes=[
            pltpu.VMEM((members * packed, width), f32),
            pltpu.SemaphoreType.DMA((3,)),
        ],
        compiler_params=pltpu.CompilerParams(vmem_limit_bytes=8 * 2**20),
    )(group, *state)


def exchange(pieces, axes):
    return lax.all_to_all(pieces, axes, 0, 0, tiled=True)


def local(grad_first, grad_second, master, first_moment, second_moment):
    inner, _, rows, width = grad_first.shape[2:]
    blocks = 2 * rows
    x = lax.axis_size("x")
    core = lax.axis_index("core")[None]
    grads = [g[0, 0].transpose(0, 2, 1, 3) for g in (grad_first, grad_second)]
    other = lax.ppermute(rows_to_send(core, *grads, x), "core", [(0, 1), (1, 0)])
    pair = add_own_rows(core, *grads, other)
    near = exchange(pair.reshape(x * 2 * Z_NEAR, -1, width), ("x", "y_near", "z_near"))
    near = fold(near, (inner // x // 2 * Z_FAR, blocks, width))
    last = exchange(near, ("y_far", "z_far"))
    state = [v.reshape(blocks, 1, width) for v in (master, first_moment, second_moment)]
    *updated, spread = update(last, *state, inner)
    codes, scales, *updated = finish(exchange(spread, INNER), updated)
    codes = codes.reshape(2, rows, inner, width).transpose(0, 2, 1, 3)
    return (
        *(v.reshape(master.shape) for v in updated),
        codes[:, :, None],
        scales.transpose(1, 2, 0)[:, :, None],
    )


def solution(mesh):
    inner, outer = mesh.devices.shape
    split = Mesh(
        mesh.devices.reshape(inner // 8, 4, 2, outer // 4, Z_NEAR, 2),
        INNER + OUTER,
    )
    return jax.shard_map(
        local,
        mesh=split,
        in_specs=(P(OUTER, INNER), P(OUTER, INNER)) + (P(None, INNER, OUTER),) * 3,
        out_specs=(P(None, INNER, OUTER),) * 3 + (P(None, None, OUTER),) * 2,
        check_vma=False,
    )
```

```python
import jax
import jax.numpy as jnp
from jax import lax
from jax.experimental import pallas as pl
from jax.experimental.pallas import tpu as pltpu
from jax.sharding import Mesh
from jax.sharding import PartitionSpec as P

EPSILON = 1e-06
CODE_RANGE = 448.0
BETA_ONE = 0.9
BETA_TWO = 0.95
LEARN_RATE = 0.01
WEIGHT_DECAY = 0.1
ADAM_EPSILON = 1e-08
steps_done = 10.0

INNER = ("x", "y_far", "y_near")
OUTER = ("z_far", "z_near", "core")
Z_FAR, Z_NEAR, OUTERS = 4, 2, 16
PACKED = 16
ANYWHERE = pl.BlockSpec(memory_space=pl.ANY)
SCALAR = pl.BlockSpec(memory_space=pltpu.SMEM)
VECTOR = pl.BlockSpec(memory_space=pltpu.VMEM)
f32, bf16 = jnp.float32, jnp.bfloat16


def adamw(reduced, params, first, second):
    first_next = BETA_ONE * first + (1.0 - BETA_ONE) * reduced
    second_next = BETA_TWO * second + (1.0 - BETA_TWO) * reduced * reduced
    first_hat = first_next / (1.0 - BETA_ONE**steps_done)
    second_hat = second_next / (1.0 - BETA_TWO**steps_done)
    params_next = params - LEARN_RATE * (
        first_hat / (jnp.sqrt(second_hat) + ADAM_EPSILON) + WEIGHT_DECAY * params
    )
    return (params_next, first_next, second_next)


def sorter(core, rows):
    half = rows * OUTERS
    to = lax.broadcasted_iota(jnp.int32, (half, 2 * half), 0)
    at = lax.broadcasted_iota(jnp.int32, (half, 2 * half), 1)
    near, far, block = (at >> 1) & (Z_NEAR - 1), (at >> 2) & (Z_FAR - 1), at >> 4
    place = near * (half // Z_NEAR) + far * (2 * rows) + block
    return jnp.where((to == place) & ((at & 1) == core), 1.0, 0.0).astype(bf16)


def sort_two(sort, first, second, a):
    half, width = first.shape[1] * first.shape[2], first.shape[3]
    columns = [
        jnp.concatenate([ref[a + n].reshape(half, width) for ref in (first, second)], axis=0)
        for n in range(2)
    ]
    return jnp.dot(sort, jnp.concatenate(columns, axis=1), preferred_element_type=f32)


def places(values, a, per_x, width):
    part = values.shape[0] // Z_NEAR
    for n in range(2):
        for z in range(Z_NEAR):
            yield (
                ((a + n) // per_x, z, (a + n) % per_x),
                values[z * part : (z + 1) * part, n * width : (n + 1) * width],
            )


def send_kernel(core_ref, first_ref, second_ref, send_ref, first, second, sem):
    inner, rows, _, width = first_ref.shape
    per_x = send_ref.shape[2]
    loads = sem.shape[0]
    span = inner // loads

    def load(i, k):
        part = pl.ds(i * span, span)
        return pltpu.make_async_copy(
            (first_ref, second_ref)[k].at[part], (first, second)[k].at[part], sem.at[i, k]
        )

    for i in range(loads):
        for k in range(2):
            load(i, k).start()
    sort = sorter(1 - core_ref[0], rows)
    for a in range(0, inner, 2):
        if a % span == 0:
            for k in range(2):
                load(a // span, k).wait()
        values = sort_two(sort, first, second, a).astype(bf16)
        for place, piece in places(values, a, per_x, width):
            send_ref[place] = piece


def rows_to_send(core, first, second, x):
    inner, rows, outer, width = first.shape
    shape = (x, Z_NEAR, inner // x, rows * outer // 2, width)
    return pl.pallas_call(
        send_kernel,
        out_shape=jax.ShapeDtypeStruct(shape, bf16),
        in_specs=[SCALAR, ANYWHERE, ANYWHERE],
        out_specs=VECTOR,
        scratch_shapes=[
            pltpu.VMEM(first.shape, bf16),
            pltpu.VMEM(first.shape, bf16),
            pltpu.SemaphoreType.DMA((2, 2)),
        ],
        compiler_params=pltpu.CompilerParams(vmem_limit_bytes=16 * 2**20),
    )(core, *(pltpu.with_memory_space_constraint(g, pltpu.HBM) for g in (first, second)))


def add_kernel(core_ref, x_ref, first_ref, second_ref, other_ref, *out_refs):
    rows, width = first_ref.shape[1], first_ref.shape[3]
    x, near, per_x, part, _ = other_ref.shape
    sort = sorter(core_ref[0], rows)
    for step, out_ref in enumerate(out_refs):
        owner = lax.rem(x_ref[0] + step, x)
        for y in range(0, per_x, 2):
            values = sort_two(sort, first_ref, second_ref, owner * per_x + y)
            for n in range(2):
                for z in range(near):
                    piece = values[z * part : (z + 1) * part, n * width : (n + 1) * width]
                    out_ref[z, y + n] = (piece + other_ref[owner, z, y + n].astype(f32)).astype(bf16)


def add_own_rows(core, my_x, first, second, other):
    piece = jax.ShapeDtypeStruct(other.shape[1:], bf16)
    return pl.pallas_call(
        add_kernel,
        out_shape=(piece,) * other.shape[0],
        in_specs=[SCALAR, SCALAR, VECTOR, VECTOR, VECTOR],
        out_specs=(VECTOR,) * other.shape[0],
        compiler_params=pltpu.CompilerParams(vmem_limit_bytes=16 * 2**20),
    )(core, my_x, first, second, other)


def fold_kernel(*refs):
    *term_refs, out_ref = refs
    near, per_x, part, _ = term_refs[0].shape
    rows = out_ref.shape[1]
    pieces = part // rows
    for z in range(near):
        for y in range(per_x):
            total = sum(ref[z, y].astype(f32) for ref in term_refs)
            for far in range(pieces):
                out_ref[(z * per_x + y) * pieces + far] = total[far * rows : (far + 1) * rows].astype(bf16)


def fold(terms, rows):
    near, per_x, part, width = terms[0].shape
    return pl.pallas_call(
        fold_kernel,
        out_shape=jax.ShapeDtypeStruct((near * per_x * part // rows, rows, width), bf16),
        in_specs=[VECTOR] * len(terms),
        out_specs=VECTOR,
        compiler_params=pltpu.CompilerParams(vmem_limit_bytes=8 * 2**20),
    )(*terms)


def update_kernel(terms_ref, master_ref, first_ref, second_ref, *out_refs):
    _, blocks, width = terms_ref.shape
    reduced = jnp.sum(terms_ref[...].astype(f32), axis=0)
    state = (
        jnp.concatenate([ref[k] for k in range(blocks)], axis=0)
        for ref in (master_ref, first_ref, second_ref)
    )
    updated = adamw(reduced, *state)
    for ref, value in zip(out_refs, updated):
        for k in range(blocks):
            ref[k] = value[k : k + 1]
    params_next = updated[0]
    largest = jnp.max(jnp.abs(params_next), axis=-1, keepdims=True)
    scale = ((largest + EPSILON) / CODE_RANGE).astype(bf16).astype(f32)
    row = lax.broadcasted_iota(jnp.int32, (blocks, width), 0)
    lane = lax.broadcasted_iota(jnp.int32, (blocks, width), 1)
    scale_row = jnp.sum(jnp.where(row == lane, scale, 0.0), axis=0, keepdims=True)
    filling = jnp.zeros((PACKED - blocks - 1, width), f32)
    packed = jnp.concatenate([params_next / scale, scale_row, filling], axis=0).astype(bf16)
    spread_ref = out_refs[3]
    for i in range(spread_ref.shape[0]):
        spread_ref[i] = packed


def update(terms, master, first, second, members):
    state = jax.ShapeDtypeStruct(master.shape, f32)
    spread = jax.ShapeDtypeStruct((members, PACKED, master.shape[-1]), bf16)
    return pl.pallas_call(
        update_kernel,
        out_shape=(state, state, state, spread),
        in_specs=[VECTOR] * 4,
        out_specs=(VECTOR,) * 4,
        compiler_params=pltpu.CompilerParams(vmem_limit_bytes=8 * 2**20),
    )(terms, master, first, second)


def unpack_kernel(group_ref, codes_ref, scales_ref, wide):
    members, packed, width = group_ref.shape
    blocks = codes_ref.shape[0]
    wide[...] = group_ref[...].astype(f32).reshape(members * packed, width)

    def row(k):
        return wide[pl.ds(k, members, stride=packed), :]

    for k in range(blocks):
        codes_ref[k] = row(k).astype(bf16)
    scales = row(blocks).T
    half = blocks // 2
    for j in range(half):
        scales_ref[j] = jnp.concatenate(
            [scales[k : k + 1] for k in (j, half + j)], axis=0
        ).astype(bf16)


def unpack(group, blocks):
    members, packed, width = group.shape
    return pl.pallas_call(
        unpack_kernel,
        out_shape=(
            jax.ShapeDtypeStruct((blocks, members, width), bf16),
            jax.ShapeDtypeStruct((blocks // 2, 2, members), bf16),
        ),
        in_specs=[VECTOR],
        out_specs=(VECTOR, VECTOR),
        scratch_shapes=[pltpu.VMEM((members * packed, width), f32)],
        compiler_params=pltpu.CompilerParams(vmem_limit_bytes=8 * 2**20),
    )(group)


def exchange(pieces, axes):
    return lax.all_to_all(pieces, axes, 0, 0, tiled=True)


def local(grad_first, grad_second, master, first_moment, second_moment):
    inner, _, rows, width = grad_first.shape[2:]
    blocks = 2 * rows
    x = lax.axis_size("x")
    core = lax.axis_index("core")[None]
    grads = [g[0, 0].transpose(0, 2, 1, 3) for g in (grad_first, grad_second)]
    other = lax.ppermute(rows_to_send(core, *grads, x), "core", [(0, 1), (1, 0)])
    mine, *others = add_own_rows(core, lax.axis_index("x")[None], *grads, other)
    terms = [mine] + [
        lax.ppermute(piece, "x", [(i, (i + step) % x) for i in range(x)])
        for step, piece in enumerate(others, start=1)
    ]
    last = exchange(fold(terms, blocks), ("z_near", "y_far", "y_near", "z_far"))
    state = [v.reshape(blocks, 1, width) for v in (master, first_moment, second_moment)]
    *updated, spread = update(last, *state, inner)
    codes, scales = unpack(exchange(spread, INNER), blocks)
    codes = codes.reshape(2, rows, inner, width).transpose(0, 2, 1, 3)
    return (
        *(v.reshape(master.shape) for v in updated),
        codes[:, :, None],
        scales.transpose(1, 2, 0)[:, :, None],
    )


def solution(mesh):
    inner, outer = mesh.devices.shape
    split = Mesh(
        mesh.devices.reshape(inner // 8, 4, 2, outer // 4, Z_NEAR, 2),
        INNER + OUTER,
    )
    return jax.shard_map(
        local,
        mesh=split,
        in_specs=(P(OUTER, INNER), P(OUTER, INNER)) + (P(None, INNER, OUTER),) * 3,
        out_specs=(P(None, INNER, OUTER),) * 3 + (P(None, None, OUTER),) * 2,
        check_vma=False,
    )
```

```python
import jax
import jax.numpy as jnp
from jax import lax
from jax.experimental import pallas as pl
from jax.experimental.pallas import tpu as pltpu
from jax.sharding import Mesh
from jax.sharding import PartitionSpec as P

EPSILON = 1e-06
CODE_RANGE = 448.0
BETA_ONE = 0.9
BETA_TWO = 0.95
LEARN_RATE = 0.01
WEIGHT_DECAY = 0.1
ADAM_EPSILON = 1e-08
steps_done = 10.0

INNER = ("x", "y_far", "y_near")
OUTER = ("z_far", "z_near", "core")
Z_FAR, Z_NEAR, OUTERS = 4, 2, 16
PACKED = 16
ANYWHERE = pl.BlockSpec(memory_space=pl.ANY)
SCALAR = pl.BlockSpec(memory_space=pltpu.SMEM)
VECTOR = pl.BlockSpec(memory_space=pltpu.VMEM)
f32, bf16 = jnp.float32, jnp.bfloat16


def adamw(reduced, params, first, second):
    first_next = BETA_ONE * first + (1.0 - BETA_ONE) * reduced
    second_next = BETA_TWO * second + (1.0 - BETA_TWO) * reduced * reduced
    first_hat = first_next / (1.0 - BETA_ONE**steps_done)
    second_hat = second_next / (1.0 - BETA_TWO**steps_done)
    params_next = params - LEARN_RATE * (
        first_hat / (jnp.sqrt(second_hat) + ADAM_EPSILON) + WEIGHT_DECAY * params
    )
    return (params_next, first_next, second_next)


def sorter(core, rows):
    half = rows * OUTERS
    to = lax.broadcasted_iota(jnp.int32, (half, 2 * half), 0)
    at = lax.broadcasted_iota(jnp.int32, (half, 2 * half), 1)
    near, far, block = (at >> 1) & (Z_NEAR - 1), (at >> 2) & (Z_FAR - 1), at >> 4
    place = near * (half // Z_NEAR) + far * (2 * rows) + block
    return jnp.where((to == place) & ((at & 1) == core), 1.0, 0.0).astype(bf16)


def sort_two(sort, first, second, a):
    half, width = first.shape[1] * first.shape[2], first.shape[3]
    columns = [
        jnp.concatenate([ref[a + n].reshape(half, width) for ref in (first, second)], axis=0)
        for n in range(2)
    ]
    return jnp.dot(sort, jnp.concatenate(columns, axis=1), preferred_element_type=f32)


def places(values, a, y_far, width):
    part = values.shape[0] // Z_NEAR
    for n in range(2):
        for z in range(Z_NEAR):
            yield (
                (a // (2 * y_far), n, z, a // 2 % y_far),
                values[z * part : (z + 1) * part, n * width : (n + 1) * width],
            )


def send_kernel(core_ref, first_ref, second_ref, send_ref, first, second, sem):
    inner, rows, _, width = first_ref.shape
    y_far = send_ref.shape[3]
    starts = (0, inner // 4 * 3)

    def load(i, k):
        part = pl.ds(starts[i], (starts + (inner,))[i + 1] - starts[i])
        return pltpu.make_async_copy(
            (first_ref, second_ref)[k].at[part], (first, second)[k].at[part], sem.at[i, k]
        )

    for i in range(len(starts)):
        for k in range(2):
            load(i, k).start()
    sort = sorter(1 - core_ref[0], rows)
    for a in range(0, inner, 2):
        if a in starts:
            for k in range(2):
                load(starts.index(a), k).wait()
        values = sort_two(sort, first, second, a).astype(bf16)
        for place, piece in places(values, a, y_far, width):
            send_ref[place] = piece


def rows_to_send(core, first, second, x):
    inner, rows, outer, width = first.shape
    shape = (x, 2, Z_NEAR, inner // x // 2, rows * outer // 2, width)
    return pl.pallas_call(
        send_kernel,
        out_shape=(
            jax.ShapeDtypeStruct(shape, bf16),
            pltpu.VMEM(first.shape, bf16),
            pltpu.VMEM(first.shape, bf16),
        ),
        in_specs=[SCALAR, ANYWHERE, ANYWHERE],
        out_specs=(VECTOR, VECTOR, VECTOR),
        scratch_shapes=[pltpu.SemaphoreType.DMA((2, 2))],
        compiler_params=pltpu.CompilerParams(vmem_limit_bytes=16 * 2**20),
    )(core, *(pltpu.with_memory_space_constraint(g, pltpu.HBM) for g in (first, second)))


def keep_kernel(core_ref, first_ref, second_ref, keep_ref):
    inner, rows, _, width = first_ref.shape
    y_far = keep_ref.shape[3]
    sort = sorter(core_ref[0], rows)
    for a in range(0, inner, 2):
        values = sort_two(sort, first_ref, second_ref, a).astype(bf16)
        for place, piece in places(values, a, y_far, width):
            keep_ref[place] = piece


def rows_to_keep(core, first, second, shape):
    return pl.pallas_call(
        keep_kernel,
        out_shape=pltpu.VMEM(shape, bf16),
        in_specs=[SCALAR, VECTOR, VECTOR],
        out_specs=VECTOR,
        compiler_params=pltpu.CompilerParams(vmem_limit_bytes=16 * 2**20),
    )(core, first, second)


def add_kernel(own_ref, other_ref, out_ref):
    for i in range(own_ref.shape[0]):
        out_ref[i] = (own_ref[i].astype(f32) + other_ref[i].astype(f32)).astype(bf16)


def add(own, other):
    return pl.pallas_call(
        add_kernel,
        out_shape=jax.ShapeDtypeStruct(own.shape, bf16),
        in_specs=[VECTOR, VECTOR],
        out_specs=VECTOR,
        compiler_params=pltpu.CompilerParams(vmem_limit_bytes=8 * 2**20),
    )(own, other)


def fold_kernel(terms_ref, out_ref):
    total = jnp.sum(terms_ref[...].astype(f32), axis=0)
    pieces, rows, _ = out_ref.shape
    for i in range(pieces):
        out_ref[i] = total[i * rows : (i + 1) * rows].astype(bf16)


def fold(terms, shape):
    return pl.pallas_call(
        fold_kernel,
        out_shape=jax.ShapeDtypeStruct(shape, bf16),
        in_specs=[VECTOR],
        out_specs=VECTOR,
        compiler_params=pltpu.CompilerParams(vmem_limit_bytes=8 * 2**20),
    )(terms)


def update_kernel(terms_ref, master_ref, first_ref, second_ref, *out_refs):
    _, blocks, width = terms_ref.shape
    reduced = jnp.sum(terms_ref[...].astype(f32), axis=0)
    state = (
        jnp.concatenate([ref[k] for k in range(blocks)], axis=0)
        for ref in (master_ref, first_ref, second_ref)
    )
    updated = adamw(reduced, *state)
    for ref, value in zip(out_refs, updated):
        for k in range(blocks):
            ref[k] = value[k : k + 1]
    params_next = updated[0]
    largest = jnp.max(jnp.abs(params_next), axis=-1, keepdims=True)
    scale = ((largest + EPSILON) / CODE_RANGE).astype(bf16).astype(f32)
    row = lax.broadcasted_iota(jnp.int32, (blocks, width), 0)
    lane = lax.broadcasted_iota(jnp.int32, (blocks, width), 1)
    scale_row = jnp.sum(jnp.where(row == lane, scale, 0.0), axis=0, keepdims=True)
    filling = jnp.zeros((PACKED - blocks - 1, width), f32)
    packed = jnp.concatenate([params_next / scale, scale_row, filling], axis=0).astype(bf16)
    spread_ref = out_refs[3]
    for i in range(spread_ref.shape[0]):
        spread_ref[i] = packed


def update(terms, master, first, second, members):
    state = jax.ShapeDtypeStruct(master.shape, f32)
    spread = jax.ShapeDtypeStruct((members, PACKED, master.shape[-1]), bf16)
    return pl.pallas_call(
        update_kernel,
        out_shape=(state, state, state, spread),
        in_specs=[VECTOR] * 4,
        out_specs=(VECTOR,) * 4,
        compiler_params=pltpu.CompilerParams(vmem_limit_bytes=8 * 2**20),
    )(terms, master, first, second)


def unpack_kernel(group_ref, codes_ref, scales_ref, wide):
    members, packed, width = group_ref.shape
    blocks = codes_ref.shape[0]
    wide[...] = group_ref[...].astype(f32).reshape(members * packed, width)

    def row(k):
        return wide[pl.ds(k, members, stride=packed), :]

    for k in range(blocks):
        codes_ref[k] = row(k).astype(bf16)
    scales = row(blocks).T
    half = blocks // 2
    for j in range(half):
        scales_ref[j] = jnp.concatenate(
            [scales[k : k + 1] for k in (j, half + j)], axis=0
        ).astype(bf16)


def unpack(group, blocks):
    members, packed, width = group.shape
    return pl.pallas_call(
        unpack_kernel,
        out_shape=(
            jax.ShapeDtypeStruct((blocks, members, width), bf16),
            jax.ShapeDtypeStruct((blocks // 2, 2, members), bf16),
        ),
        in_specs=[VECTOR],
        out_specs=(VECTOR, VECTOR),
        scratch_shapes=[pltpu.VMEM((members * packed, width), f32)],
        compiler_params=pltpu.CompilerParams(vmem_limit_bytes=8 * 2**20),
    )(group)


def exchange(pieces, axes):
    return lax.all_to_all(pieces, axes, 0, 0, tiled=True)


def local(grad_first, grad_second, master, first_moment, second_moment):
    inner, _, rows, width = grad_first.shape[2:]
    blocks = 2 * rows
    x = lax.axis_size("x")
    core = lax.axis_index("core")[None]
    grads = [g[0, 0].transpose(0, 2, 1, 3) for g in (grad_first, grad_second)]
    send, *grads = rows_to_send(core, *grads, x)
    other = lax.ppermute(send, "core", [(0, 1), (1, 0)])
    pair = add(rows_to_keep(core, *grads, send.shape), other)
    near = exchange(pair.reshape(x * 2 * Z_NEAR, -1, width), ("x", "y_near", "z_near"))
    near = fold(near, (inner // x // 2 * Z_FAR, blocks, width))
    last = exchange(near, ("y_far", "z_far"))
    state = [v.reshape(blocks, 1, width) for v in (master, first_moment, second_moment)]
    *updated, spread = update(last, *state, inner)
    codes, scales = unpack(exchange(spread, INNER), blocks)
    codes = codes.reshape(2, rows, inner, width).transpose(0, 2, 1, 3)
    return (
        *(v.reshape(master.shape) for v in updated),
        codes[:, :, None],
        scales.transpose(1, 2, 0)[:, :, None],
    )


def solution(mesh):
    inner, outer = mesh.devices.shape
    split = Mesh(
        mesh.devices.reshape(inner // 8, 4, 2, outer // 4, Z_NEAR, 2),
        INNER + OUTER,
    )
    return jax.shard_map(
        local,
        mesh=split,
        in_specs=(P(OUTER, INNER), P(OUTER, INNER)) + (P(None, INNER, OUTER),) * 3,
        out_specs=(P(None, INNER, OUTER),) * 3 + (P(None, None, OUTER),) * 2,
        check_vma=False,
    )
```

```python
import functools

import jax
import jax.numpy as jnp
from jax import lax
from jax.experimental import pallas as pl
from jax.experimental.pallas import tpu as pltpu
from jax.sharding import Mesh
from jax.sharding import PartitionSpec as P

EPSILON = 1e-06
CODE_RANGE = 448.0
BETA_ONE = 0.9
BETA_TWO = 0.95
LEARN_RATE = 0.01
WEIGHT_DECAY = 0.1
ADAM_EPSILON = 1e-08
steps_done = 10.0

INNER = ("x", "y_far", "y_near")
OUTER = ("z_far", "z_near", "core")
Z_FAR, Z_NEAR, OUTERS = 4, 2, 16
PACKED = 16
ANYWHERE = pl.BlockSpec(memory_space=pl.ANY)
SCALAR = pl.BlockSpec(memory_space=pltpu.SMEM)
VECTOR = pl.BlockSpec(memory_space=pltpu.VMEM)
f32, bf16 = jnp.float32, jnp.bfloat16


def adamw(reduced, params, first, second):
    first_next = BETA_ONE * first + (1.0 - BETA_ONE) * reduced
    second_next = BETA_TWO * second + (1.0 - BETA_TWO) * reduced * reduced
    first_hat = first_next / (1.0 - BETA_ONE**steps_done)
    second_hat = second_next / (1.0 - BETA_TWO**steps_done)
    params_next = params - LEARN_RATE * (
        first_hat / (jnp.sqrt(second_hat) + ADAM_EPSILON) + WEIGHT_DECAY * params
    )
    return (params_next, first_next, second_next)


def sorter(core, rows):
    half = rows * OUTERS
    to = lax.broadcasted_iota(jnp.int32, (half, 2 * half), 0)
    at = lax.broadcasted_iota(jnp.int32, (half, 2 * half), 1)
    near, far, block = (at >> 1) & (Z_NEAR - 1), (at >> 2) & (Z_FAR - 1), at >> 4
    place = near * (half // Z_NEAR) + far * (2 * rows) + block
    return jnp.where((to == place) & ((at & 1) == core), 1.0, 0.0).astype(bf16)


def sort_two(sort, first, second, a):
    half, width = first.shape[1] * first.shape[2], first.shape[3]
    columns = [
        jnp.concatenate([ref[a + n].reshape(half, width) for ref in (first, second)], axis=0)
        for n in range(2)
    ]
    return jnp.dot(sort, jnp.concatenate(columns, axis=1), preferred_element_type=f32)


def places(values, a, y_far, width):
    part = values.shape[0] // Z_NEAR
    for n in range(2):
        for z in range(Z_NEAR):
            yield (
                (n, z, a // (2 * y_far), a // 2 % y_far),
                values[z * part : (z + 1) * part, n * width : (n + 1) * width],
            )


def send_kernel(core_ref, first_ref, second_ref, send_ref, first, second, sem):
    inner, rows, _, width = first_ref.shape
    y_far = send_ref.shape[3]
    starts = (0, inner // 4 * 3)

    def load(i, k):
        part = pl.ds(starts[i], (starts + (inner,))[i + 1] - starts[i])
        return pltpu.make_async_copy(
            (first_ref, second_ref)[k].at[part], (first, second)[k].at[part], sem.at[i, k]
        )

    for i in range(len(starts)):
        for k in range(2):
            load(i, k).start()
    sort = sorter(1 - core_ref[0], rows)
    for a in range(0, inner, 2):
        if a in starts:
            for k in range(2):
                load(starts.index(a), k).wait()
        values = sort_two(sort, first, second, a).astype(bf16)
        for place, piece in places(values, a, y_far, width):
            send_ref[place] = piece


def rows_to_send(core, first, second, x):
    inner, rows, outer, width = first.shape
    shape = (2, Z_NEAR, x, inner // x // 2, rows * outer // 2, width)
    return pl.pallas_call(
        send_kernel,
        out_shape=(
            jax.ShapeDtypeStruct(shape, bf16),
            pltpu.VMEM(first.shape, bf16),
            pltpu.VMEM(first.shape, bf16),
        ),
        in_specs=[SCALAR, ANYWHERE, ANYWHERE],
        out_specs=(VECTOR, VECTOR, VECTOR),
        scratch_shapes=[pltpu.SemaphoreType.DMA((2, 2))],
        compiler_params=pltpu.CompilerParams(vmem_limit_bytes=16 * 2**20),
    )(core, *(pltpu.with_memory_space_constraint(g, pltpu.HBM) for g in (first, second)))


def keep_kernel(core_ref, first_ref, second_ref, keep_ref):
    inner, rows, _, width = first_ref.shape
    y_far = keep_ref.shape[3]
    sort = sorter(core_ref[0], rows)
    for a in range(0, inner, 2):
        values = sort_two(sort, first_ref, second_ref, a).astype(bf16)
        for place, piece in places(values, a, y_far, width):
            keep_ref[place] = piece


def rows_to_keep(core, first, second, shape):
    return pl.pallas_call(
        keep_kernel,
        out_shape=pltpu.VMEM(shape, bf16),
        in_specs=[SCALAR, VECTOR, VECTOR],
        out_specs=VECTOR,
        compiler_params=pltpu.CompilerParams(vmem_limit_bytes=16 * 2**20),
    )(core, first, second)


def add_kernel(own_ref, other_ref, out_ref):
    for i in range(own_ref.shape[0]):
        out_ref[i] = (own_ref[i].astype(f32) + other_ref[i].astype(f32)).astype(bf16)


def add(own, other):
    return pl.pallas_call(
        add_kernel,
        out_shape=jax.ShapeDtypeStruct(own.shape, bf16),
        in_specs=[VECTOR, VECTOR],
        out_specs=VECTOR,
        compiler_params=pltpu.CompilerParams(vmem_limit_bytes=8 * 2**20),
    )(own, other)


def fold_kernel(terms_ref, out_ref):
    total = jnp.sum(terms_ref[...].astype(f32), axis=0)
    pieces, rows, _ = out_ref.shape
    for i in range(pieces):
        out_ref[i] = total[i * rows : (i + 1) * rows].astype(bf16)


def fold(terms, shape):
    return pl.pallas_call(
        fold_kernel,
        out_shape=jax.ShapeDtypeStruct(shape, bf16),
        in_specs=[VECTOR],
        out_specs=VECTOR,
        compiler_params=pltpu.CompilerParams(vmem_limit_bytes=8 * 2**20),
    )(terms)


def update_kernel(terms_ref, master_ref, first_ref, second_ref, *out_refs):
    _, blocks, width = terms_ref.shape
    reduced = jnp.sum(terms_ref[...].astype(f32), axis=0)
    state = (
        jnp.concatenate([ref[k] for k in range(blocks)], axis=0)
        for ref in (master_ref, first_ref, second_ref)
    )
    updated = adamw(reduced, *state)
    for ref, value in zip(out_refs, updated):
        for k in range(blocks):
            ref[k] = value[k : k + 1]
    params_next = updated[0]
    largest = jnp.max(jnp.abs(params_next), axis=-1, keepdims=True)
    scale = ((largest + EPSILON) / CODE_RANGE).astype(bf16).astype(f32)
    row = lax.broadcasted_iota(jnp.int32, (blocks, width), 0)
    lane = lax.broadcasted_iota(jnp.int32, (blocks, width), 1)
    scale_row = jnp.sum(jnp.where(row == lane, scale, 0.0), axis=0, keepdims=True)
    filling = jnp.zeros((PACKED - blocks - 1, width), f32)
    packed = jnp.concatenate([params_next / scale, scale_row, filling], axis=0).astype(bf16)
    spread_ref = out_refs[3]
    for i in range(spread_ref.shape[0]):
        spread_ref[i] = packed


def update(terms, master, first, second, members):
    state = jax.ShapeDtypeStruct(master.shape, f32)
    spread = jax.ShapeDtypeStruct((members, PACKED, master.shape[-1]), bf16)
    return pl.pallas_call(
        update_kernel,
        out_shape=(state, state, state, spread),
        in_specs=[VECTOR] * 4,
        out_specs=(VECTOR,) * 4,
        compiler_params=pltpu.CompilerParams(vmem_limit_bytes=8 * 2**20),
    )(terms, master, first, second)


def unpack_kernel(xs, group_ref, codes_ref, scales_ref, wide):
    members, packed, width = group_ref.shape
    blocks = codes_ref.shape[0]
    wide[...] = group_ref[...].astype(f32).reshape(members * packed, width)

    def row(k):
        return jnp.concatenate(
            [wide[pl.ds(x * packed + k, members // xs, stride=xs * packed), :] for x in range(xs)],
            axis=0,
        )

    for k in range(blocks):
        codes_ref[k] = row(k).astype(bf16)
    scales = row(blocks).T
    half = blocks // 2
    for j in range(half):
        scales_ref[j] = jnp.concatenate(
            [scales[k : k + 1] for k in (j, half + j)], axis=0
        ).astype(bf16)


def unpack(group, blocks, xs):
    members, packed, width = group.shape
    return pl.pallas_call(
        functools.partial(unpack_kernel, xs),
        out_shape=(
            jax.ShapeDtypeStruct((blocks, members, width), bf16),
            jax.ShapeDtypeStruct((blocks // 2, 2, members), bf16),
        ),
        in_specs=[VECTOR],
        out_specs=(VECTOR, VECTOR),
        scratch_shapes=[pltpu.VMEM((members * packed, width), f32)],
        compiler_params=pltpu.CompilerParams(vmem_limit_bytes=8 * 2**20),
    )(group)


def exchange(pieces, axes):
    return lax.all_to_all(pieces, axes, 0, 0, tiled=True)


def local(grad_first, grad_second, master, first_moment, second_moment):
    inner, _, rows, width = grad_first.shape[2:]
    blocks = 2 * rows
    x = lax.axis_size("x")
    core = lax.axis_index("core")[None]
    grads = [g[0, 0].transpose(0, 2, 1, 3) for g in (grad_first, grad_second)]
    send, *grads = rows_to_send(core, *grads, x)
    other = lax.ppermute(send, "core", [(0, 1), (1, 0)])
    pair = add(rows_to_keep(core, *grads, send.shape), other)
    near = exchange(pair.reshape(x * 2 * Z_NEAR, -1, width), ("y_near", "z_near", "x"))
    near = fold(near, (inner // x // 2 * Z_FAR, blocks, width))
    last = exchange(near, ("y_far", "z_far"))
    state = [v.reshape(blocks, 1, width) for v in (master, first_moment, second_moment)]
    *updated, spread = update(last, *state, inner)
    codes, scales = unpack(exchange(spread, ("y_far", "y_near", "x")), blocks, x)
    codes = codes.reshape(2, rows, inner, width).transpose(0, 2, 1, 3)
    return (
        *(v.reshape(master.shape) for v in updated),
        codes[:, :, None],
        scales.transpose(1, 2, 0)[:, :, None],
    )


def solution(mesh):
    inner, outer = mesh.devices.shape
    split = Mesh(
        mesh.devices.reshape(inner // 8, 4, 2, outer // 4, Z_NEAR, 2),
        INNER + OUTER,
    )
    return jax.shard_map(
        local,
        mesh=split,
        in_specs=(P(OUTER, INNER), P(OUTER, INNER)) + (P(None, INNER, OUTER),) * 3,
        out_specs=(P(None, INNER, OUTER),) * 3 + (P(None, None, OUTER),) * 2,
        check_vma=False,
    )
```

```python
import jax
import jax.numpy as jnp
from jax import lax
from jax.experimental import pallas as pl
from jax.experimental.pallas import tpu as pltpu
from jax.sharding import Mesh
from jax.sharding import PartitionSpec as P

EPSILON = 1e-06
CODE_RANGE = 448.0
BETA_ONE = 0.9
BETA_TWO = 0.95
LEARN_RATE = 0.01
WEIGHT_DECAY = 0.1
ADAM_EPSILON = 1e-08
steps_done = 10.0

INNER = ("x", "y_far", "y_near")
OUTER = ("z_far", "z_near", "core")
Z_FAR, Z_NEAR, OUTERS = 4, 2, 16
PACKED = 16
ANYWHERE = pl.BlockSpec(memory_space=pl.ANY)
SCALAR = pl.BlockSpec(memory_space=pltpu.SMEM)
VECTOR = pl.BlockSpec(memory_space=pltpu.VMEM)
f32, bf16 = jnp.float32, jnp.bfloat16


def adamw(reduced, params, first, second):
    first_next = BETA_ONE * first + (1.0 - BETA_ONE) * reduced
    second_next = BETA_TWO * second + (1.0 - BETA_TWO) * reduced * reduced
    first_hat = first_next / (1.0 - BETA_ONE**steps_done)
    second_hat = second_next / (1.0 - BETA_TWO**steps_done)
    params_next = params - LEARN_RATE * (
        first_hat / (jnp.sqrt(second_hat) + ADAM_EPSILON) + WEIGHT_DECAY * params
    )
    return (params_next, first_next, second_next)


def sorter(core, rows):
    half = rows * OUTERS
    to = lax.broadcasted_iota(jnp.int32, (half, 2 * half), 0)
    at = lax.broadcasted_iota(jnp.int32, (half, 2 * half), 1)
    near, far, block = (at >> 1) & (Z_NEAR - 1), (at >> 2) & (Z_FAR - 1), at >> 4
    place = near * (half // Z_NEAR) + far * (2 * rows) + block
    return jnp.where((to == place) & ((at & 1) == core), 1.0, 0.0).astype(bf16)


def sort_two(sort, first, second, a):
    half, width = first.shape[1] * first.shape[2], first.shape[3]
    columns = [
        jnp.concatenate([ref[a + n].reshape(half, width) for ref in (first, second)], axis=0)
        for n in range(2)
    ]
    return jnp.dot(sort, jnp.concatenate(columns, axis=1), preferred_element_type=f32)


def places(values, a, y_far, width):
    part = values.shape[0] // Z_NEAR
    for n in range(2):
        for z in range(Z_NEAR):
            yield (
                (a // (2 * y_far), n, z, a // 2 % y_far),
                values[z * part : (z + 1) * part, n * width : (n + 1) * width],
            )


def send_kernel(core_ref, first_ref, second_ref, send_ref, first, second, sem):
    inner, rows, _, width = first_ref.shape
    y_far = send_ref.shape[3]
    starts = (0, inner // 4 * 3)

    def load(i, k):
        part = pl.ds(starts[i], (starts + (inner,))[i + 1] - starts[i])
        return pltpu.make_async_copy(
            (first_ref, second_ref)[k].at[part], (first, second)[k].at[part], sem.at[i, k]
        )

    for i in range(len(starts)):
        for k in range(2):
            load(i, k).start()
    sort = sorter(1 - core_ref[0], rows)
    for a in range(0, inner, 2):
        if a in starts:
            for k in range(2):
                load(starts.index(a), k).wait()
        values = sort_two(sort, first, second, a).astype(bf16)
        for place, piece in places(values, a, y_far, width):
            send_ref[place] = piece


def rows_to_send(core, first, second, x):
    inner, rows, outer, width = first.shape
    shape = (x, 2, Z_NEAR, inner // x // 2, rows * outer // 2, width)
    return pl.pallas_call(
        send_kernel,
        out_shape=(
            jax.ShapeDtypeStruct(shape, bf16),
            pltpu.VMEM(first.shape, bf16),
            pltpu.VMEM(first.shape, bf16),
        ),
        in_specs=[SCALAR, ANYWHERE, ANYWHERE],
        out_specs=(VECTOR, VECTOR, VECTOR),
        scratch_shapes=[pltpu.SemaphoreType.DMA((2, 2))],
        compiler_params=pltpu.CompilerParams(vmem_limit_bytes=16 * 2**20),
    )(core, *(pltpu.with_memory_space_constraint(g, pltpu.HBM) for g in (first, second)))


def keep_kernel(core_ref, first_ref, second_ref, keep_ref):
    inner, rows, _, width = first_ref.shape
    y_far = keep_ref.shape[3]
    sort = sorter(core_ref[0], rows)
    for a in range(0, inner, 2):
        values = sort_two(sort, first_ref, second_ref, a).astype(bf16)
        for place, piece in places(values, a, y_far, width):
            keep_ref[place] = piece


def rows_to_keep(core, first, second, shape):
    return pl.pallas_call(
        keep_kernel,
        out_shape=pltpu.VMEM(shape, bf16),
        in_specs=[SCALAR, VECTOR, VECTOR],
        out_specs=VECTOR,
        compiler_params=pltpu.CompilerParams(vmem_limit_bytes=16 * 2**20),
    )(core, first, second)


def add_kernel(own_ref, other_ref, out_ref):
    for i in range(own_ref.shape[0]):
        out_ref[i] = (own_ref[i].astype(f32) + other_ref[i].astype(f32)).astype(bf16)


def add(own, other):
    return pl.pallas_call(
        add_kernel,
        out_shape=jax.ShapeDtypeStruct(own.shape, bf16),
        in_specs=[VECTOR, VECTOR],
        out_specs=VECTOR,
        compiler_params=pltpu.CompilerParams(vmem_limit_bytes=8 * 2**20),
    )(own, other)


def fold_kernel(terms_ref, out_ref):
    total = jnp.sum(terms_ref[...].astype(f32), axis=0)
    pieces, rows, _ = out_ref.shape
    for i in range(pieces):
        out_ref[i] = total[i * rows : (i + 1) * rows].astype(bf16)


def fold(terms, shape):
    return pl.pallas_call(
        fold_kernel,
        out_shape=jax.ShapeDtypeStruct(shape, bf16),
        in_specs=[VECTOR],
        out_specs=VECTOR,
        compiler_params=pltpu.CompilerParams(vmem_limit_bytes=8 * 2**20),
    )(terms)


def update_kernel(terms_ref, master_ref, first_ref, second_ref, *out_refs):
    _, blocks, width = terms_ref.shape
    reduced = jnp.sum(terms_ref[...].astype(f32), axis=0)
    state = (
        jnp.concatenate([ref[k] for k in range(blocks)], axis=0)
        for ref in (master_ref, first_ref, second_ref)
    )
    updated = adamw(reduced, *state)
    for ref, value in zip(out_refs, updated):
        for k in range(blocks):
            ref[k] = value[k : k + 1]
    params_next = updated[0]
    largest = jnp.max(jnp.abs(params_next), axis=-1, keepdims=True)
    scale = ((largest + EPSILON) / CODE_RANGE).astype(bf16).astype(f32)
    row = lax.broadcasted_iota(jnp.int32, (blocks, width), 0)
    lane = lax.broadcasted_iota(jnp.int32, (blocks, width), 1)
    scale_row = jnp.sum(jnp.where(row == lane, scale, 0.0), axis=0, keepdims=True)
    filling = jnp.zeros((PACKED - blocks - 1, width), f32)
    packed = jnp.concatenate([params_next / scale, scale_row, filling], axis=0).astype(bf16)
    spread_ref = out_refs[3]
    for i in range(spread_ref.shape[0]):
        spread_ref[i] = packed


def update(terms, master, first, second, members):
    state = pltpu.VMEM(master.shape, f32)
    spread = jax.ShapeDtypeStruct((members, PACKED, master.shape[-1]), bf16)
    return pl.pallas_call(
        update_kernel,
        out_shape=(state, state, state, spread),
        in_specs=[VECTOR] * 4,
        out_specs=(VECTOR,) * 4,
        compiler_params=pltpu.CompilerParams(vmem_limit_bytes=8 * 2**20),
    )(terms, master, first, second)


def unpack_kernel(group_ref, codes_ref, scales_ref, wide):
    members, packed, width = group_ref.shape
    blocks = codes_ref.shape[0]
    wide[...] = group_ref[...].astype(f32).reshape(members * packed, width)

    def row(k):
        return wide[pl.ds(k, members, stride=packed), :]

    for k in range(blocks):
        codes_ref[k] = row(k).astype(bf16)
    scales = row(blocks).T
    half = blocks // 2
    for j in range(half):
        scales_ref[j] = jnp.concatenate(
            [scales[k : k + 1] for k in (j, half + j)], axis=0
        ).astype(bf16)


def unpack(group, blocks):
    members, packed, width = group.shape
    return pl.pallas_call(
        unpack_kernel,
        out_shape=(
            jax.ShapeDtypeStruct((blocks, members, width), bf16),
            jax.ShapeDtypeStruct((blocks // 2, 2, members), bf16),
        ),
        in_specs=[VECTOR],
        out_specs=(VECTOR, VECTOR),
        scratch_shapes=[pltpu.VMEM((members * packed, width), f32)],
        compiler_params=pltpu.CompilerParams(vmem_limit_bytes=8 * 2**20),
    )(group)


def exchange(pieces, axes):
    return lax.all_to_all(pieces, axes, 0, 0, tiled=True)


def local(grad_first, grad_second, master, first_moment, second_moment):
    inner, _, rows, width = grad_first.shape[2:]
    blocks = 2 * rows
    x = lax.axis_size("x")
    core = lax.axis_index("core")[None]
    grads = [g[0, 0].transpose(0, 2, 1, 3) for g in (grad_first, grad_second)]
    send, *grads = rows_to_send(core, *grads, x)
    other = lax.ppermute(send, "core", [(0, 1), (1, 0)])
    pair = add(rows_to_keep(core, *grads, send.shape), other)
    near = exchange(pair.reshape(x * 2 * Z_NEAR, -1, width), ("x", "y_near", "z_near"))
    near = fold(near, (inner // x // 2 * Z_FAR, blocks, width))
    last = exchange(near, ("y_far", "z_far"))
    state = [v.reshape(blocks, 1, width) for v in (master, first_moment, second_moment)]
    *updated, spread = update(last, *state, inner)
    codes, scales = unpack(exchange(spread, INNER), blocks)
    codes = codes.reshape(2, rows, inner, width).transpose(0, 2, 1, 3)
    return (
        *(v.reshape(master.shape) for v in updated),
        codes[:, :, None],
        scales.transpose(1, 2, 0)[:, :, None],
    )


def solution(mesh):
    inner, outer = mesh.devices.shape
    split = Mesh(
        mesh.devices.reshape(inner // 8, 4, 2, outer // 4, Z_NEAR, 2),
        INNER + OUTER,
    )
    return jax.shard_map(
        local,
        mesh=split,
        in_specs=(P(OUTER, INNER), P(OUTER, INNER)) + (P(None, INNER, OUTER),) * 3,
        out_specs=(P(None, INNER, OUTER),) * 3 + (P(None, None, OUTER),) * 2,
        check_vma=False,
    )
```

```python
import jax
import jax.numpy as jnp
from jax import lax
from jax.experimental import pallas as pl
from jax.experimental.pallas import tpu as pltpu
from jax.sharding import Mesh
from jax.sharding import PartitionSpec as P

EPSILON = 1e-06
CODE_RANGE = 448.0
BETA_ONE = 0.9
BETA_TWO = 0.95
LEARN_RATE = 0.01
WEIGHT_DECAY = 0.1
ADAM_EPSILON = 1e-08
steps_done = 10.0

INNER = ("x", "y_far", "y_near")
OUTER = ("z_far", "z_near", "core")
Z_FAR, Z_NEAR, OUTERS = 4, 2, 16
PACKED = 16
ANYWHERE = pl.BlockSpec(memory_space=pl.ANY)
SCALAR = pl.BlockSpec(memory_space=pltpu.SMEM)
VECTOR = pl.BlockSpec(memory_space=pltpu.VMEM)
f32, bf16 = jnp.float32, jnp.bfloat16


def adamw(reduced, params, first, second):
    first_next = BETA_ONE * first + (1.0 - BETA_ONE) * reduced
    second_next = BETA_TWO * second + (1.0 - BETA_TWO) * reduced * reduced
    first_hat = first_next / (1.0 - BETA_ONE**steps_done)
    second_hat = second_next / (1.0 - BETA_TWO**steps_done)
    params_next = params - LEARN_RATE * (
        first_hat / (jnp.sqrt(second_hat) + ADAM_EPSILON) + WEIGHT_DECAY * params
    )
    return (params_next, first_next, second_next)


def sorter(core, rows):
    half = rows * OUTERS
    to = lax.broadcasted_iota(jnp.int32, (half, 2 * half), 0)
    at = lax.broadcasted_iota(jnp.int32, (half, 2 * half), 1)
    near, far, block = (at >> 1) & (Z_NEAR - 1), (at >> 2) & (Z_FAR - 1), at >> 4
    place = near * (half // Z_NEAR) + far * (2 * rows) + block
    return jnp.where((to == place) & ((at & 1) == core), 1.0, 0.0).astype(bf16)


def sort_two(sort, first, second, a):
    half, width = first.shape[1] * first.shape[2], first.shape[3]
    columns = [
        jnp.concatenate([ref[a + n].reshape(half, width) for ref in (first, second)], axis=0)
        for n in range(2)
    ]
    return jnp.dot(sort, jnp.concatenate(columns, axis=1), preferred_element_type=f32)


def places(values, a, ys, width):
    part = values.shape[0] // Z_NEAR
    for n in range(2):
        for z in range(Z_NEAR):
            yield (
                ((a + n) // ys, z, (a + n) % ys),
                values[z * part : (z + 1) * part, n * width : (n + 1) * width],
            )


def send_kernel(core_ref, first_ref, second_ref, send_ref, first, second, sem):
    inner, rows, _, width = first_ref.shape
    ys = send_ref.shape[2]
    starts = (0, inner // 4 * 3)

    def load(i, k):
        part = pl.ds(starts[i], (starts + (inner,))[i + 1] - starts[i])
        return pltpu.make_async_copy(
            (first_ref, second_ref)[k].at[part], (first, second)[k].at[part], sem.at[i, k]
        )

    for i in range(len(starts)):
        for k in range(2):
            load(i, k).start()
    sort = sorter(1 - core_ref[0], rows)
    for a in range(0, inner, 2):
        if a in starts:
            for k in range(2):
                load(starts.index(a), k).wait()
        values = sort_two(sort, first, second, a).astype(bf16)
        for place, piece in places(values, a, ys, width):
            send_ref[place] = piece


def rows_to_send(core, first, second, x):
    inner, rows, outer, width = first.shape
    shape = (x, Z_NEAR, inner // x, rows * outer // 2, width)
    return pl.pallas_call(
        send_kernel,
        out_shape=(
            jax.ShapeDtypeStruct(shape, bf16),
            pltpu.VMEM(first.shape, bf16),
            pltpu.VMEM(first.shape, bf16),
        ),
        in_specs=[SCALAR, ANYWHERE, ANYWHERE],
        out_specs=(VECTOR, VECTOR, VECTOR),
        scratch_shapes=[pltpu.SemaphoreType.DMA((2, 2))],
        compiler_params=pltpu.CompilerParams(vmem_limit_bytes=16 * 2**20),
    )(core, *(pltpu.with_memory_space_constraint(g, pltpu.HBM) for g in (first, second)))


def keep_kernel(core_ref, first_ref, second_ref, keep_ref):
    inner, rows, _, width = first_ref.shape
    ys = keep_ref.shape[2]
    sort = sorter(core_ref[0], rows)
    for a in range(0, inner, 2):
        values = sort_two(sort, first_ref, second_ref, a).astype(bf16)
        for place, piece in places(values, a, ys, width):
            keep_ref[place] = piece


def rows_to_keep(core, first, second, shape):
    return pl.pallas_call(
        keep_kernel,
        out_shape=pltpu.VMEM(shape, bf16),
        in_specs=[SCALAR, VECTOR, VECTOR],
        out_specs=VECTOR,
        compiler_params=pltpu.CompilerParams(vmem_limit_bytes=16 * 2**20),
    )(core, first, second)


def add_kernel(own_ref, other_ref, out_ref):
    for i in range(own_ref.shape[0]):
        out_ref[i] = (own_ref[i].astype(f32) + other_ref[i].astype(f32)).astype(bf16)


def add(own, other):
    return pl.pallas_call(
        add_kernel,
        out_shape=jax.ShapeDtypeStruct(own.shape, bf16),
        in_specs=[VECTOR, VECTOR],
        out_specs=VECTOR,
        compiler_params=pltpu.CompilerParams(vmem_limit_bytes=8 * 2**20),
    )(own, other)


def fold_kernel(terms_ref, out_ref):
    total = jnp.sum(terms_ref[...].astype(f32), axis=0)
    pieces, rows, _ = out_ref.shape
    for i in range(pieces):
        out_ref[i] = total[i * rows : (i + 1) * rows].astype(bf16)


def fold(terms, shape):
    return pl.pallas_call(
        fold_kernel,
        out_shape=jax.ShapeDtypeStruct(shape, bf16),
        in_specs=[VECTOR],
        out_specs=VECTOR,
        compiler_params=pltpu.CompilerParams(vmem_limit_bytes=8 * 2**20),
    )(terms)


def update_kernel(terms_ref, master_ref, first_ref, second_ref, *out_refs):
    _, blocks, width = terms_ref.shape
    reduced = jnp.sum(terms_ref[...].astype(f32), axis=0)
    state = (
        jnp.concatenate([ref[k] for k in range(blocks)], axis=0)
        for ref in (master_ref, first_ref, second_ref)
    )
    updated = adamw(reduced, *state)
    for ref, value in zip(out_refs, updated):
        for k in range(blocks):
            ref[k] = value[k : k + 1]
    params_next = updated[0]
    largest = jnp.max(jnp.abs(params_next), axis=-1, keepdims=True)
    scale = ((largest + EPSILON) / CODE_RANGE).astype(bf16).astype(f32)
    row = lax.broadcasted_iota(jnp.int32, (blocks, width), 0)
    lane = lax.broadcasted_iota(jnp.int32, (blocks, width), 1)
    scale_row = jnp.sum(jnp.where(row == lane, scale, 0.0), axis=0, keepdims=True)
    filling = jnp.zeros((PACKED - blocks - 1, width), f32)
    packed = jnp.concatenate([params_next / scale, scale_row, filling], axis=0).astype(bf16)
    spread_ref = out_refs[3]
    for i in range(spread_ref.shape[0]):
        spread_ref[i] = packed


def update(terms, master, first, second, members):
    state = jax.ShapeDtypeStruct(master.shape, f32)
    spread = jax.ShapeDtypeStruct((members, PACKED, master.shape[-1]), bf16)
    return pl.pallas_call(
        update_kernel,
        out_shape=(state, state, state, spread),
        in_specs=[VECTOR] * 4,
        out_specs=(VECTOR,) * 4,
        compiler_params=pltpu.CompilerParams(vmem_limit_bytes=8 * 2**20),
    )(terms, master, first, second)


def unpack_kernel(group_ref, codes_ref, scales_ref, wide):
    members, packed, width = group_ref.shape
    blocks = codes_ref.shape[0]
    wide[...] = group_ref[...].astype(f32).reshape(members * packed, width)

    def row(k):
        return wide[pl.ds(k, members, stride=packed), :]

    for k in range(blocks):
        codes_ref[k] = row(k).astype(bf16)
    scales = row(blocks).T
    half = blocks // 2
    for j in range(half):
        scales_ref[j] = jnp.concatenate(
            [scales[k : k + 1] for k in (j, half + j)], axis=0
        ).astype(bf16)


def unpack(group, blocks):
    members, packed, width = group.shape
    return pl.pallas_call(
        unpack_kernel,
        out_shape=(
            jax.ShapeDtypeStruct((blocks, members, width), bf16),
            jax.ShapeDtypeStruct((blocks // 2, 2, members), bf16),
        ),
        in_specs=[VECTOR],
        out_specs=(VECTOR, VECTOR),
        scratch_shapes=[pltpu.VMEM((members * packed, width), f32)],
        compiler_params=pltpu.CompilerParams(vmem_limit_bytes=8 * 2**20),
    )(group)


def exchange(pieces, axes):
    return lax.all_to_all(pieces, axes, 0, 0, tiled=True)


def local(grad_first, grad_second, master, first_moment, second_moment):
    inner, _, rows, width = grad_first.shape[2:]
    blocks = 2 * rows
    x = lax.axis_size("x")
    core = lax.axis_index("core")[None]
    grads = [g[0, 0].transpose(0, 2, 1, 3) for g in (grad_first, grad_second)]
    send, *grads = rows_to_send(core, *grads, x)
    other = lax.ppermute(send, "core", [(0, 1), (1, 0)])
    pair = add(rows_to_keep(core, *grads, send.shape), other)
    cross = exchange(pair.reshape(x * Z_NEAR, -1, width), ("x", "z_near"))
    cross = fold(cross, (inner // x * Z_FAR, blocks, width))
    last = exchange(cross, ("y_far", "y_near", "z_far"))
    state = [v.reshape(blocks, 1, width) for v in (master, first_moment, second_moment)]
    *updated, spread = update(last, *state, inner)
    codes, scales = unpack(exchange(spread, INNER), blocks)
    codes = codes.reshape(2, rows, inner, width).transpose(0, 2, 1, 3)
    return (
        *(v.reshape(master.shape) for v in updated),
        codes[:, :, None],
        scales.transpose(1, 2, 0)[:, :, None],
    )


def solution(mesh):
    inner, outer = mesh.devices.shape
    split = Mesh(
        mesh.devices.reshape(inner // 8, 4, 2, outer // 4, Z_NEAR, 2),
        INNER + OUTER,
    )
    return jax.shard_map(
        local,
        mesh=split,
        in_specs=(P(OUTER, INNER), P(OUTER, INNER)) + (P(None, INNER, OUTER),) * 3,
        out_specs=(P(None, INNER, OUTER),) * 3 + (P(None, None, OUTER),) * 2,
        check_vma=False,
    )
```

```python
import jax
import jax.numpy as jnp
from jax import lax
from jax.experimental import pallas as pl
from jax.experimental.pallas import tpu as pltpu
from jax.sharding import Mesh
from jax.sharding import PartitionSpec as P

EPSILON = 1e-06
CODE_RANGE = 448.0
BETA_ONE = 0.9
BETA_TWO = 0.95
LEARN_RATE = 0.01
WEIGHT_DECAY = 0.1
ADAM_EPSILON = 1e-08
steps_done = 10.0

INNER = ("x", "y_far", "y_near")
OUTER = ("z_far", "z_near", "core")
Z_FAR, Z_NEAR, OUTERS = 4, 2, 16
PACKED = 16
ANYWHERE = pl.BlockSpec(memory_space=pl.ANY)
SCALAR = pl.BlockSpec(memory_space=pltpu.SMEM)
VECTOR = pl.BlockSpec(memory_space=pltpu.VMEM)
f32, bf16 = jnp.float32, jnp.bfloat16


def adamw(reduced, params, first, second):
    first_next = BETA_ONE * first + (1.0 - BETA_ONE) * reduced
    second_next = BETA_TWO * second + (1.0 - BETA_TWO) * reduced * reduced
    first_hat = first_next / (1.0 - BETA_ONE**steps_done)
    second_hat = second_next / (1.0 - BETA_TWO**steps_done)
    params_next = params - LEARN_RATE * (
        first_hat / (jnp.sqrt(second_hat) + ADAM_EPSILON) + WEIGHT_DECAY * params
    )
    return (params_next, first_next, second_next)


def sorter(core, rows):
    half = rows * OUTERS
    to = lax.broadcasted_iota(jnp.int32, (half, 2 * half), 0)
    at = lax.broadcasted_iota(jnp.int32, (half, 2 * half), 1)
    near, far, block = (at >> 1) & (Z_NEAR - 1), (at >> 2) & (Z_FAR - 1), at >> 4
    place = near * (half // Z_NEAR) + far * (2 * rows) + block
    return jnp.where((to == place) & ((at & 1) == core), 1.0, 0.0).astype(bf16)


def sort_two(sort, first, second, a):
    half, width = first.shape[1] * first.shape[2], first.shape[3]
    columns = [
        jnp.concatenate([ref[a + n].reshape(half, width) for ref in (first, second)], axis=0)
        for n in range(2)
    ]
    return jnp.dot(sort, jnp.concatenate(columns, axis=1), preferred_element_type=f32)


def places(values, a, y_far, width):
    part = values.shape[0] // Z_NEAR
    for n in range(2):
        for z in range(Z_NEAR):
            yield (
                (a // (2 * y_far), n, z, a // 2 % y_far),
                values[z * part : (z + 1) * part, n * width : (n + 1) * width],
            )


def send_kernel(core_ref, first_ref, second_ref, send_ref, first, second, sem):
    inner, rows, _, width = first_ref.shape
    y_far = send_ref.shape[3]
    starts = (0, inner // 4 * 3)

    def load(i, k):
        part = pl.ds(starts[i], (starts + (inner,))[i + 1] - starts[i])
        return pltpu.make_async_copy(
            (first_ref, second_ref)[k].at[part], (first, second)[k].at[part], sem.at[i, k]
        )

    for i in range(len(starts)):
        for k in range(2):
            load(i, k).start()
    sort = sorter(1 - core_ref[0], rows)
    for a in range(0, inner, 2):
        if a in starts:
            for k in range(2):
                load(starts.index(a), k).wait()
        values = sort_two(sort, first, second, a).astype(bf16)
        for place, piece in places(values, a, y_far, width):
            send_ref[place] = piece


def rows_to_send(core, first, second, x):
    inner, rows, outer, width = first.shape
    shape = (x, 2, Z_NEAR, inner // x // 2, rows * outer // 2, width)
    return pl.pallas_call(
        send_kernel,
        out_shape=(
            jax.ShapeDtypeStruct(shape, bf16),
            pltpu.VMEM(first.shape, bf16),
            pltpu.VMEM(first.shape, bf16),
        ),
        in_specs=[SCALAR, ANYWHERE, ANYWHERE],
        out_specs=(VECTOR, VECTOR, VECTOR),
        scratch_shapes=[pltpu.SemaphoreType.DMA((2, 2))],
        compiler_params=pltpu.CompilerParams(vmem_limit_bytes=16 * 2**20),
    )(core, *(pltpu.with_memory_space_constraint(g, pltpu.HBM) for g in (first, second)))


def keep_kernel(core_ref, first_ref, second_ref, keep_ref):
    inner, rows, _, width = first_ref.shape
    y_far = keep_ref.shape[3]
    sort = sorter(core_ref[0], rows)
    for a in range(0, inner, 2):
        values = sort_two(sort, first_ref, second_ref, a).astype(bf16)
        for place, piece in places(values, a, y_far, width):
            keep_ref[place] = piece


def rows_to_keep(core, first, second, shape):
    return pl.pallas_call(
        keep_kernel,
        out_shape=pltpu.VMEM(shape, bf16),
        in_specs=[SCALAR, VECTOR, VECTOR],
        out_specs=VECTOR,
        compiler_params=pltpu.CompilerParams(vmem_limit_bytes=16 * 2**20),
    )(core, first, second)


def add_kernel(own_ref, other_ref, out_ref):
    for i in range(own_ref.shape[0]):
        out_ref[i] = (own_ref[i].astype(f32) + other_ref[i].astype(f32)).astype(bf16)


def add(own, other):
    return pl.pallas_call(
        add_kernel,
        out_shape=jax.ShapeDtypeStruct(own.shape, bf16),
        in_specs=[VECTOR, VECTOR],
        out_specs=VECTOR,
        compiler_params=pltpu.CompilerParams(vmem_limit_bytes=8 * 2**20),
    )(own, other)


def fold_kernel(terms_ref, out_ref):
    total = jnp.sum(terms_ref[...].astype(f32), axis=0)
    pieces, rows, _ = out_ref.shape
    for i in range(pieces):
        out_ref[i] = total[i * rows : (i + 1) * rows].astype(bf16)


def fold(terms, shape):
    return pl.pallas_call(
        fold_kernel,
        out_shape=jax.ShapeDtypeStruct(shape, bf16),
        in_specs=[VECTOR],
        out_specs=VECTOR,
        compiler_params=pltpu.CompilerParams(vmem_limit_bytes=8 * 2**20),
    )(terms)


def update_kernel(terms_ref, master_ref, first_ref, second_ref, *out_refs):
    _, blocks, width = terms_ref.shape
    reduced = jnp.sum(terms_ref[...].astype(f32), axis=0)
    state = (
        jnp.concatenate([ref[k] for k in range(blocks)], axis=0)
        for ref in (master_ref, first_ref, second_ref)
    )
    updated = adamw(reduced, *state)
    for ref, value in zip(out_refs, updated):
        for k in range(blocks):
            ref[k] = value[k : k + 1]
    params_next = updated[0]
    largest = jnp.max(jnp.abs(params_next), axis=-1, keepdims=True)
    scale = ((largest + EPSILON) / CODE_RANGE).astype(bf16).astype(f32)
    row = lax.broadcasted_iota(jnp.int32, (blocks, width), 0)
    lane = lax.broadcasted_iota(jnp.int32, (blocks, width), 1)
    scale_row = jnp.sum(jnp.where(row == lane, scale, 0.0), axis=0, keepdims=True)
    filling = jnp.zeros((PACKED - blocks - 1, width), f32)
    packed = jnp.concatenate([params_next / scale, scale_row, filling], axis=0).astype(bf16)
    spread_ref = out_refs[3]
    for i in range(spread_ref.shape[0]):
        spread_ref[i] = packed


def update(terms, master, first, second, members):
    state = pltpu.VMEM(master.shape, f32)
    spread = pltpu.VMEM((members, PACKED, master.shape[-1]), bf16)
    return pl.pallas_call(
        update_kernel,
        out_shape=(state, state, state, spread),
        in_specs=[VECTOR] * 4,
        out_specs=(VECTOR,) * 4,
        compiler_params=pltpu.CompilerParams(vmem_limit_bytes=8 * 2**20),
    )(terms, master, first, second)


def finish_kernel(group_ref, *refs):
    state_refs, (codes_ref, scales_ref), stored_refs, wide = refs[:3], refs[3:5], refs[5:8], refs[8]
    for new_ref, stored_ref in zip(state_refs, stored_refs):
        stored_ref[...] = new_ref[...]
    members, packed, width = group_ref.shape
    blocks = codes_ref.shape[0]
    wide[...] = group_ref[...].astype(f32).reshape(members * packed, width)

    def row(k):
        return wide[pl.ds(k, members, stride=packed), :]

    for k in range(blocks):
        codes_ref[k] = row(k).astype(bf16)
    scales = row(blocks).T
    half = blocks // 2
    for j in range(half):
        scales_ref[j] = jnp.concatenate(
            [scales[k : k + 1] for k in (j, half + j)], axis=0
        ).astype(bf16)


def finish(group, state):
    members, packed, width = group.shape
    blocks = state[0].shape[0]
    stored = jax.ShapeDtypeStruct(state[0].shape, f32)
    return pl.pallas_call(
        finish_kernel,
        out_shape=(
            jax.ShapeDtypeStruct((blocks, members, width), bf16),
            jax.ShapeDtypeStruct((blocks // 2, 2, members), bf16),
            stored,
            stored,
            stored,
        ),
        in_specs=[VECTOR] * 4,
        out_specs=(VECTOR,) * 5,
        scratch_shapes=[pltpu.VMEM((members * packed, width), f32)],
        compiler_params=pltpu.CompilerParams(vmem_limit_bytes=8 * 2**20),
    )(group, *state)


def exchange(pieces, axes):
    return lax.all_to_all(pieces, axes, 0, 0, tiled=True)


def local(grad_first, grad_second, master, first_moment, second_moment):
    inner, _, rows, width = grad_first.shape[2:]
    blocks = 2 * rows
    x = lax.axis_size("x")
    core = lax.axis_index("core")[None]
    grads = [g[0, 0].transpose(0, 2, 1, 3) for g in (grad_first, grad_second)]
    send, *grads = rows_to_send(core, *grads, x)
    other = lax.ppermute(send, "core", [(0, 1), (1, 0)])
    pair = add(rows_to_keep(core, *grads, send.shape), other)
    near = exchange(pair.reshape(x * 2 * Z_NEAR, -1, width), ("x", "y_near", "z_near"))
    near = fold(near, (inner // x // 2 * Z_FAR, blocks, width))
    last = exchange(near, ("y_far", "z_far"))
    state = [v.reshape(blocks, 1, width) for v in (master, first_moment, second_moment)]
    *updated, spread = update(last, *state, inner)
    codes, scales, *updated = finish(exchange(spread, INNER), updated)
    codes = codes.reshape(2, rows, inner, width).transpose(0, 2, 1, 3)
    return (
        *(v.reshape(master.shape) for v in updated),
        codes[:, :, None],
        scales.transpose(1, 2, 0)[:, :, None],
    )


def solution(mesh):
    inner, outer = mesh.devices.shape
    split = Mesh(
        mesh.devices.reshape(inner // 8, 4, 2, outer // 4, Z_NEAR, 2),
        INNER + OUTER,
    )
    return jax.shard_map(
        local,
        mesh=split,
        in_specs=(P(OUTER, INNER), P(OUTER, INNER)) + (P(None, INNER, OUTER),) * 3,
        out_specs=(P(None, INNER, OUTER),) * 3 + (P(None, None, OUTER),) * 2,
        check_vma=False,
    )
```

```python
import jax
import jax.numpy as jnp
from jax import lax
from jax.experimental import pallas as pl
from jax.experimental.pallas import tpu as pltpu
from jax.sharding import Mesh
from jax.sharding import PartitionSpec as P

EPSILON = 1e-06
CODE_RANGE = 448.0
BETA_ONE = 0.9
BETA_TWO = 0.95
LEARN_RATE = 0.01
WEIGHT_DECAY = 0.1
ADAM_EPSILON = 1e-08
steps_done = 10.0

INNER = ("x", "y_far", "y_near")
OUTER = ("z_far", "z_near", "core")
Z_FAR, Z_NEAR, OUTERS = 4, 2, 16
PACKED = 16
ANYWHERE = pl.BlockSpec(memory_space=pl.ANY)
SCALAR = pl.BlockSpec(memory_space=pltpu.SMEM)
VECTOR = pl.BlockSpec(memory_space=pltpu.VMEM)
f32, bf16 = jnp.float32, jnp.bfloat16


def adamw(reduced, params, first, second):
    first_next = BETA_ONE * first + (1.0 - BETA_ONE) * reduced
    second_next = BETA_TWO * second + (1.0 - BETA_TWO) * reduced * reduced
    first_hat = first_next / (1.0 - BETA_ONE**steps_done)
    second_hat = second_next / (1.0 - BETA_TWO**steps_done)
    params_next = params - LEARN_RATE * (
        first_hat / (jnp.sqrt(second_hat) + ADAM_EPSILON) + WEIGHT_DECAY * params
    )
    return (params_next, first_next, second_next)


def sorter(core, rows):
    half = rows * OUTERS
    to = lax.broadcasted_iota(jnp.int32, (half, 2 * half), 0)
    at = lax.broadcasted_iota(jnp.int32, (half, 2 * half), 1)
    near, far, block = (at >> 1) & (Z_NEAR - 1), (at >> 2) & (Z_FAR - 1), at >> 4
    place = near * (half // Z_NEAR) + far * (2 * rows) + block
    return jnp.where((to == place) & ((at & 1) == core), 1.0, 0.0).astype(bf16)


def sort_two(sort, first, second, a):
    half, width = first.shape[1] * first.shape[2], first.shape[3]
    columns = [
        jnp.concatenate([ref[a + n].reshape(half, width) for ref in (first, second)], axis=0)
        for n in range(2)
    ]
    return jnp.dot(sort, jnp.concatenate(columns, axis=1), preferred_element_type=f32)


def places(values, a, ys, width):
    part = values.shape[0] // Z_NEAR
    for n in range(2):
        for z in range(Z_NEAR):
            yield (
                ((a + n) // ys, z, (a + n) % ys),
                values[z * part : (z + 1) * part, n * width : (n + 1) * width],
            )


def send_kernel(core_ref, first_ref, second_ref, send_ref, first, second, sem):
    inner, rows, _, width = first_ref.shape
    ys = send_ref.shape[2]
    starts = (0, inner // 4 * 3)

    def load(i, k):
        part = pl.ds(starts[i], (starts + (inner,))[i + 1] - starts[i])
        return pltpu.make_async_copy(
            (first_ref, second_ref)[k].at[part], (first, second)[k].at[part], sem.at[i, k]
        )

    for i in range(len(starts)):
        for k in range(2):
            load(i, k).start()
    sort = sorter(1 - core_ref[0], rows)
    for a in range(0, inner, 2):
        if a in starts:
            for k in range(2):
                load(starts.index(a), k).wait()
        values = sort_two(sort, first, second, a).astype(bf16)
        for place, piece in places(values, a, ys, width):
            send_ref[place] = piece


def rows_to_send(core, first, second, x):
    inner, rows, outer, width = first.shape
    shape = (x, Z_NEAR, inner // x, rows * outer // 2, width)
    return pl.pallas_call(
        send_kernel,
        out_shape=(
            jax.ShapeDtypeStruct(shape, bf16),
            pltpu.VMEM(first.shape, bf16),
            pltpu.VMEM(first.shape, bf16),
        ),
        in_specs=[SCALAR, ANYWHERE, ANYWHERE],
        out_specs=(VECTOR, VECTOR, VECTOR),
        scratch_shapes=[pltpu.SemaphoreType.DMA((2, 2))],
        compiler_params=pltpu.CompilerParams(vmem_limit_bytes=16 * 2**20),
    )(core, *(pltpu.with_memory_space_constraint(g, pltpu.HBM) for g in (first, second)))


def keep_kernel(core_ref, first_ref, second_ref, keep_ref):
    inner, rows, _, width = first_ref.shape
    ys = keep_ref.shape[2]
    sort = sorter(core_ref[0], rows)
    for a in range(0, inner, 2):
        values = sort_two(sort, first_ref, second_ref, a).astype(bf16)
        for place, piece in places(values, a, ys, width):
            keep_ref[place] = piece


def rows_to_keep(core, first, second, shape):
    return pl.pallas_call(
        keep_kernel,
        out_shape=pltpu.VMEM(shape, bf16),
        in_specs=[SCALAR, VECTOR, VECTOR],
        out_specs=VECTOR,
        compiler_params=pltpu.CompilerParams(vmem_limit_bytes=16 * 2**20),
    )(core, first, second)


def add_kernel(own_ref, other_ref, out_ref):
    for i in range(own_ref.shape[0]):
        out_ref[i] = (own_ref[i].astype(f32) + other_ref[i].astype(f32)).astype(bf16)


def add(own, other):
    return pl.pallas_call(
        add_kernel,
        out_shape=jax.ShapeDtypeStruct(own.shape, bf16),
        in_specs=[VECTOR, VECTOR],
        out_specs=VECTOR,
        compiler_params=pltpu.CompilerParams(vmem_limit_bytes=8 * 2**20),
    )(own, other)


def fold_kernel(terms_ref, out_ref):
    total = jnp.sum(terms_ref[...].astype(f32), axis=0)
    pieces, rows, _ = out_ref.shape
    for i in range(pieces):
        out_ref[i] = total[i * rows : (i + 1) * rows].astype(bf16)


def fold(terms, shape):
    return pl.pallas_call(
        fold_kernel,
        out_shape=jax.ShapeDtypeStruct(shape, bf16),
        in_specs=[VECTOR],
        out_specs=VECTOR,
        compiler_params=pltpu.CompilerParams(vmem_limit_bytes=8 * 2**20),
    )(terms)


def update_kernel(terms_ref, master_ref, first_ref, second_ref, *out_refs):
    _, blocks, width = terms_ref.shape
    reduced = jnp.sum(terms_ref[...].astype(f32), axis=0)
    state = (
        jnp.concatenate([ref[k] for k in range(blocks)], axis=0)
        for ref in (master_ref, first_ref, second_ref)
    )
    updated = adamw(reduced, *state)
    for ref, value in zip(out_refs, updated):
        for k in range(blocks):
            ref[k] = value[k : k + 1]
    params_next = updated[0]
    largest = jnp.max(jnp.abs(params_next), axis=-1, keepdims=True)
    scale = ((largest + EPSILON) / CODE_RANGE).astype(bf16).astype(f32)
    row = lax.broadcasted_iota(jnp.int32, (blocks, width), 0)
    lane = lax.broadcasted_iota(jnp.int32, (blocks, width), 1)
    scale_row = jnp.sum(jnp.where(row == lane, scale, 0.0), axis=0, keepdims=True)
    filling = jnp.zeros((PACKED - blocks - 1, width), f32)
    packed = jnp.concatenate([params_next / scale, scale_row, filling], axis=0).astype(bf16)
    spread_ref = out_refs[3]
    for i in range(spread_ref.shape[0]):
        spread_ref[i] = packed


def update(terms, master, first, second, members):
    state = pltpu.VMEM(master.shape, f32)
    spread = pltpu.VMEM((members, PACKED, master.shape[-1]), bf16)
    return pl.pallas_call(
        update_kernel,
        out_shape=(state, state, state, spread),
        in_specs=[VECTOR] * 4,
        out_specs=(VECTOR,) * 4,
        compiler_params=pltpu.CompilerParams(vmem_limit_bytes=8 * 2**20),
    )(terms, master, first, second)


def finish_kernel(group_ref, *refs):
    state_refs, (codes_ref, scales_ref), stored_refs, wide = refs[:3], refs[3:5], refs[5:8], refs[8]
    for new_ref, stored_ref in zip(state_refs, stored_refs):
        stored_ref[...] = new_ref[...]
    members, packed, width = group_ref.shape
    blocks = codes_ref.shape[0]
    wide[...] = group_ref[...].astype(f32).reshape(members * packed, width)

    def row(k):
        return wide[pl.ds(k, members, stride=packed), :]

    for k in range(blocks):
        codes_ref[k] = row(k).astype(bf16)
    scales = row(blocks).T
    half = blocks // 2
    for j in range(half):
        scales_ref[j] = jnp.concatenate(
            [scales[k : k + 1] for k in (j, half + j)], axis=0
        ).astype(bf16)


def finish(group, state):
    members, packed, width = group.shape
    blocks = state[0].shape[0]
    stored = jax.ShapeDtypeStruct(state[0].shape, f32)
    return pl.pallas_call(
        finish_kernel,
        out_shape=(
            jax.ShapeDtypeStruct((blocks, members, width), bf16),
            jax.ShapeDtypeStruct((blocks // 2, 2, members), bf16),
            stored,
            stored,
            stored,
        ),
        in_specs=[VECTOR] * 4,
        out_specs=(VECTOR,) * 5,
        scratch_shapes=[pltpu.VMEM((members * packed, width), f32)],
        compiler_params=pltpu.CompilerParams(vmem_limit_bytes=8 * 2**20),
    )(group, *state)


def exchange(pieces, axes):
    return lax.all_to_all(pieces, axes, 0, 0, tiled=True)


def local(grad_first, grad_second, master, first_moment, second_moment):
    inner, _, rows, width = grad_first.shape[2:]
    blocks = 2 * rows
    x = lax.axis_size("x")
    core = lax.axis_index("core")[None]
    grads = [g[0, 0].transpose(0, 2, 1, 3) for g in (grad_first, grad_second)]
    send, *grads = rows_to_send(core, *grads, x)
    other = lax.ppermute(send, "core", [(0, 1), (1, 0)])
    pair = add(rows_to_keep(core, *grads, send.shape), other)
    cross = exchange(pair.reshape(x * Z_NEAR, -1, width), ("x", "z_near"))
    cross = fold(cross, (inner // x * Z_FAR, blocks, width))
    last = exchange(cross, ("y_far", "y_near", "z_far"))
    state = [v.reshape(blocks, 1, width) for v in (master, first_moment, second_moment)]
    *updated, spread = update(last, *state, inner)
    codes, scales, *updated = finish(exchange(spread, INNER), updated)
    codes = codes.reshape(2, rows, inner, width).transpose(0, 2, 1, 3)
    return (
        *(v.reshape(master.shape) for v in updated),
        codes[:, :, None],
        scales.transpose(1, 2, 0)[:, :, None],
    )


def solution(mesh):
    inner, outer = mesh.devices.shape
    split = Mesh(
        mesh.devices.reshape(inner // 8, 4, 2, outer // 4, Z_NEAR, 2),
        INNER + OUTER,
    )
    return jax.shard_map(
        local,
        mesh=split,
        in_specs=(P(OUTER, INNER), P(OUTER, INNER)) + (P(None, INNER, OUTER),) * 3,
        out_specs=(P(None, INNER, OUTER),) * 3 + (P(None, None, OUTER),) * 2,
        check_vma=False,
    )
```

```python
import jax
import jax.numpy as jnp
from jax import lax
from jax.experimental import pallas as pl
from jax.experimental.pallas import tpu as pltpu
from jax.sharding import Mesh
from jax.sharding import PartitionSpec as P

EPSILON = 1e-06
CODE_RANGE = 448.0
BETA_ONE = 0.9
BETA_TWO = 0.95
LEARN_RATE = 0.01
WEIGHT_DECAY = 0.1
ADAM_EPSILON = 1e-08
steps_done = 10.0

INNER = ("x", "y_far", "y_near")
OUTER = ("z_far", "z_near", "core")
Z_FAR, Z_NEAR, OUTERS = 4, 2, 16
PACKED = 16
ANYWHERE = pl.BlockSpec(memory_space=pl.ANY)
SCALAR = pl.BlockSpec(memory_space=pltpu.SMEM)
VECTOR = pl.BlockSpec(memory_space=pltpu.VMEM)
f32, bf16 = jnp.float32, jnp.bfloat16


def adamw(reduced, params, first, second):
    first_next = BETA_ONE * first + (1.0 - BETA_ONE) * reduced
    second_next = BETA_TWO * second + (1.0 - BETA_TWO) * reduced * reduced
    first_hat = first_next / (1.0 - BETA_ONE**steps_done)
    second_hat = second_next / (1.0 - BETA_TWO**steps_done)
    params_next = params - LEARN_RATE * (
        first_hat / (jnp.sqrt(second_hat) + ADAM_EPSILON) + WEIGHT_DECAY * params
    )
    return (params_next, first_next, second_next)


def sorter(core, rows):
    half = rows * OUTERS
    to = lax.broadcasted_iota(jnp.int32, (half, 2 * half), 0)
    at = lax.broadcasted_iota(jnp.int32, (half, 2 * half), 1)
    near, far, block = (at >> 1) & (Z_NEAR - 1), (at >> 2) & (Z_FAR - 1), at >> 4
    place = near * (half // Z_NEAR) + far * (2 * rows) + block
    return jnp.where((to == place) & ((at & 1) == core), 1.0, 0.0).astype(bf16)


def sort_two(sort, first, second, a):
    half, width = first.shape[1] * first.shape[2], first.shape[3]
    columns = [
        jnp.concatenate([ref[a + n].reshape(half, width) for ref in (first, second)], axis=0)
        for n in range(2)
    ]
    return jnp.dot(sort, jnp.concatenate(columns, axis=1), preferred_element_type=f32)


def places(values, a, ys, width):
    part = values.shape[0] // Z_NEAR
    for n in range(2):
        for z in range(Z_NEAR):
            yield (
                ((a + n) // ys, z, (a + n) % ys),
                values[z * part : (z + 1) * part, n * width : (n + 1) * width],
            )


def send_kernel(core_ref, first_ref, second_ref, send_ref, first, second, sem):
    inner, rows, _, width = first_ref.shape
    ys = send_ref.shape[2]
    starts = (0, inner // 2, inner // 8 * 7)

    def load(i, k):
        part = pl.ds(starts[i], (starts + (inner,))[i + 1] - starts[i])
        return pltpu.make_async_copy(
            (first_ref, second_ref)[k].at[part], (first, second)[k].at[part], sem.at[i, k]
        )

    for i in range(len(starts)):
        for k in range(2):
            load(i, k).start()
    sort = sorter(1 - core_ref[0], rows)
    for a in range(0, inner, 2):
        if a in starts:
            for k in range(2):
                load(starts.index(a), k).wait()
        values = sort_two(sort, first, second, a).astype(bf16)
        for place, piece in places(values, a, ys, width):
            send_ref[place] = piece


def rows_to_send(core, first, second, x):
    inner, rows, outer, width = first.shape
    shape = (x, Z_NEAR, inner // x, rows * outer // 2, width)
    return pl.pallas_call(
        send_kernel,
        out_shape=(
            jax.ShapeDtypeStruct(shape, bf16),
            pltpu.VMEM(first.shape, bf16),
            pltpu.VMEM(first.shape, bf16),
        ),
        in_specs=[SCALAR, ANYWHERE, ANYWHERE],
        out_specs=(VECTOR, VECTOR, VECTOR),
        scratch_shapes=[pltpu.SemaphoreType.DMA((3, 2))],
        compiler_params=pltpu.CompilerParams(vmem_limit_bytes=16 * 2**20),
    )(core, *(pltpu.with_memory_space_constraint(g, pltpu.HBM) for g in (first, second)))


def keep_kernel(core_ref, first_ref, second_ref, keep_ref):
    inner, rows, _, width = first_ref.shape
    ys = keep_ref.shape[2]
    sort = sorter(core_ref[0], rows)
    for a in range(0, inner, 2):
        values = sort_two(sort, first_ref, second_ref, a).astype(bf16)
        for place, piece in places(values, a, ys, width):
            keep_ref[place] = piece


def rows_to_keep(core, first, second, shape):
    return pl.pallas_call(
        keep_kernel,
        out_shape=pltpu.VMEM(shape, bf16),
        in_specs=[SCALAR, VECTOR, VECTOR],
        out_specs=VECTOR,
        compiler_params=pltpu.CompilerParams(vmem_limit_bytes=16 * 2**20),
    )(core, first, second)


def add_kernel(own_ref, other_ref, out_ref):
    for i in range(own_ref.shape[0]):
        out_ref[i] = (own_ref[i].astype(f32) + other_ref[i].astype(f32)).astype(bf16)


def add(own, other):
    return pl.pallas_call(
        add_kernel,
        out_shape=jax.ShapeDtypeStruct(own.shape, bf16),
        in_specs=[VECTOR, VECTOR],
        out_specs=VECTOR,
        compiler_params=pltpu.CompilerParams(vmem_limit_bytes=8 * 2**20),
    )(own, other)


def fold_kernel(terms_ref, out_ref):
    total = jnp.sum(terms_ref[...].astype(f32), axis=0)
    pieces, rows, _ = out_ref.shape
    for i in range(pieces):
        out_ref[i] = total[i * rows : (i + 1) * rows].astype(bf16)


def fold(terms, shape):
    return pl.pallas_call(
        fold_kernel,
        out_shape=jax.ShapeDtypeStruct(shape, bf16),
        in_specs=[VECTOR],
        out_specs=VECTOR,
        compiler_params=pltpu.CompilerParams(vmem_limit_bytes=8 * 2**20),
    )(terms)


def update_kernel(terms_ref, master_ref, first_ref, second_ref, *out_refs):
    _, blocks, width = terms_ref.shape
    reduced = jnp.sum(terms_ref[...].astype(f32), axis=0)
    state = (
        jnp.concatenate([ref[k] for k in range(blocks)], axis=0)
        for ref in (master_ref, first_ref, second_ref)
    )
    updated = adamw(reduced, *state)
    for ref, value in zip(out_refs, updated):
        for k in range(blocks):
            ref[k] = value[k : k + 1]
    params_next = updated[0]
    largest = jnp.max(jnp.abs(params_next), axis=-1, keepdims=True)
    scale = ((largest + EPSILON) / CODE_RANGE).astype(bf16).astype(f32)
    row = lax.broadcasted_iota(jnp.int32, (blocks, width), 0)
    lane = lax.broadcasted_iota(jnp.int32, (blocks, width), 1)
    scale_row = jnp.sum(jnp.where(row == lane, scale, 0.0), axis=0, keepdims=True)
    filling = jnp.zeros((PACKED - blocks - 1, width), f32)
    packed = jnp.concatenate([params_next / scale, scale_row, filling], axis=0).astype(bf16)
    spread_ref = out_refs[3]
    for i in range(spread_ref.shape[0]):
        spread_ref[i] = packed


def update(terms, master, first, second, members):
    state = pltpu.VMEM(master.shape, f32)
    spread = pltpu.VMEM((members, PACKED, master.shape[-1]), bf16)
    return pl.pallas_call(
        update_kernel,
        out_shape=(state, state, state, spread),
        in_specs=[VECTOR] * 4,
        out_specs=(VECTOR,) * 4,
        compiler_params=pltpu.CompilerParams(vmem_limit_bytes=8 * 2**20),
    )(terms, master, first, second)


def finish_kernel(group_ref, *refs):
    state_refs, (codes_ref, scales_ref), stored_refs, wide = refs[:3], refs[3:5], refs[5:8], refs[8]
    for new_ref, stored_ref in zip(state_refs, stored_refs):
        stored_ref[...] = new_ref[...]
    members, packed, width = group_ref.shape
    blocks = codes_ref.shape[0]
    wide[...] = group_ref[...].astype(f32).reshape(members * packed, width)

    def row(k):
        return wide[pl.ds(k, members, stride=packed), :]

    for k in range(blocks):
        codes_ref[k] = row(k).astype(bf16)
    scales = row(blocks).T
    half = blocks // 2
    for j in range(half):
        scales_ref[j] = jnp.concatenate(
            [scales[k : k + 1] for k in (j, half + j)], axis=0
        ).astype(bf16)


def finish(group, state):
    members, packed, width = group.shape
    blocks = state[0].shape[0]
    stored = jax.ShapeDtypeStruct(state[0].shape, f32)
    return pl.pallas_call(
        finish_kernel,
        out_shape=(
            jax.ShapeDtypeStruct((blocks, members, width), bf16),
            jax.ShapeDtypeStruct((blocks // 2, 2, members), bf16),
            stored,
            stored,
            stored,
        ),
        in_specs=[VECTOR] * 4,
        out_specs=(VECTOR,) * 5,
        scratch_shapes=[pltpu.VMEM((members * packed, width), f32)],
        compiler_params=pltpu.CompilerParams(vmem_limit_bytes=8 * 2**20),
    )(group, *state)


def exchange(pieces, axes):
    return lax.all_to_all(pieces, axes, 0, 0, tiled=True)


def local(grad_first, grad_second, master, first_moment, second_moment):
    inner, _, rows, width = grad_first.shape[2:]
    blocks = 2 * rows
    x = lax.axis_size("x")
    core = lax.axis_index("core")[None]
    grads = [g[0, 0].transpose(0, 2, 1, 3) for g in (grad_first, grad_second)]
    send, *grads = rows_to_send(core, *grads, x)
    other = lax.ppermute(send, "core", [(0, 1), (1, 0)])
    pair = add(rows_to_keep(core, *grads, send.shape), other)
    cross = exchange(pair.reshape(x * Z_NEAR, -1, width), ("x", "z_near"))
    cross = fold(cross, (inner // x * Z_FAR, blocks, width))
    last = exchange(cross, ("y_far", "y_near", "z_far"))
    state = [v.reshape(blocks, 1, width) for v in (master, first_moment, second_moment)]
    *updated, spread = update(last, *state, inner)
    codes, scales, *updated = finish(exchange(spread, INNER), updated)
    codes = codes.reshape(2, rows, inner, width).transpose(0, 2, 1, 3)
    return (
        *(v.reshape(master.shape) for v in updated),
        codes[:, :, None],
        scales.transpose(1, 2, 0)[:, :, None],
    )


def solution(mesh):
    inner, outer = mesh.devices.shape
    split = Mesh(
        mesh.devices.reshape(inner // 8, 4, 2, outer // 4, Z_NEAR, 2),
        INNER + OUTER,
    )
    return jax.shard_map(
        local,
        mesh=split,
        in_specs=(P(OUTER, INNER), P(OUTER, INNER)) + (P(None, INNER, OUTER),) * 3,
        out_specs=(P(None, INNER, OUTER),) * 3 + (P(None, None, OUTER),) * 2,
        check_vma=False,
    )
```
